128 devices in a mesh: aper: 16 (over y, x_hi, core), swath: 8 (over z, x_lo).
Axes of the slice: x: 4 (x_hi: 2, x_lo: 2; x = x_hi * 2 + x_lo), y: 4, z: 4, core: 2. Of those that a mesh axis runs over, the one named last changes fastest.
Arguments:
- polar_field: float32 [2, 2048, 8192], P(None, 'aper', 'swath'), may hold values from -6 to 6
- tap_index: int32 [3, 16, 2, 8, 128], P(None, 'aper'), may hold values from 0 to 127
- tap_weight: float32 [3, 16, 2, 8, 128], P(None, 'aper'), may hold values from -1.5 to 1.5
- range_shift: float32 [3, 16, 2, 128], P(None, 'aper'), may hold values from -8 to 8
- range_gain: float32 [3, 8192], P(None, 'swath'), may hold values from 0.1 to 1.9
- tile_owner: int32 [16, 8, 8, 1], P('aper', 'swath'), may hold values from 0 to 15; in each aligned block of 8 rows (0 to 7, 8 to 15, ..., all dimensions but the last counted through in order) at most 2 rows name the same one
- block_weights: float32 [16, 8, 8, 128, 128], P('aper', 'swath'), may hold values from -0.5 to 0.5
- kernel_index: int32 [16, 8], P('aper', 'swath'), may hold values from 0 to 15
- kernel_bank: float32 [16, 81], replicated, may hold values from -0.625 to 0.625
Outputs:
- deconvolved: float32 [2, 2048, 1024], P(None, 'aper', 'swath')
The draws below stay inside these ranges and needn't reach their ends.
Inputs may be any that keep to these rules, and one draw needn't show every extreme that they name: `tile_owner`: the 8 polar blocks of one device name any one owner at most 2 times, and some device names one owner exactly 2 times; every owner is named somewhere.
All inputs are finite; a program needn't handle non-finite values.
Results may differ from the reference program's by a relative error of at most 0.00011.
Values sent between devices are 32-bit elements; how exact they have to be, the bound alone decides.
No kernel may reach another device: no remote copies, remote signals or barrier semaphores. Data moves between devices by JAX's collectives and lax.ppermute only.
A program may use at most 128 MiB of HBM per device.

```python
import math
import jax
import jax.numpy as jnp
import numpy as np
from jax import lax

ANGLES = 128
RANGE_BINS = 1024
TAPS = 8
SECTIONS = 3
BLOCK_BINS = 128
TILE_ROWS = 128
SLOTS = 2
KERNELS = 16
N_APER = 16
N_SWATH = 8


def with_ends(values, rng, least, high):
    longest = values.shape.index(max(values.shape))
    spots = []
    for shift in (0, 1):
        where = [jax.random.randint(jax.random.fold_in(rng, axis), (), 0, length) for axis, length in enumerate(values.shape)]
        where[longest] = (where[longest] + shift) % values.shape[longest]
        spots.append(tuple(where))
    return values.at[spots[0]].set(least).at[spots[1]].set(high)


def block_levels(key, extent, shards, smallest, top_value):
    gain, own = 1.0, jax.random.fold_in(key, 6)
    for axis_at, blocks in shards:
        steps = jnp.exp(jax.random.uniform(jax.random.fold_in(own, axis_at), (blocks,), jnp.float32, smallest / len(shards), top_value / len(shards)))
        gain = gain * jnp.repeat(steps, extent[axis_at] // blocks).reshape([-1 if axis == axis_at else 1 for axis in range(len(extent))])
    return gain


def shared_out(stream_key, own, number, rows, amount, top, reach, slope):
    order = jax.random.permutation(stream_key, amount)
    crowded, ordinary = load_shares(amount, rows * top, reach, slope, True), load_shares(amount, rows * top, reach, slope, False)
    places = jnp.arange(amount)

    def named(lengths, rotation):
        used = int((lengths > 0).sum())
        fixed = max(1, used // 4)
        passed = fixed + (places - fixed + rotation * (used - fixed)) % max(1, amount - fixed)
        return jnp.zeros((amount,), jnp.int32).at[order[jnp.where(places < fixed, places, passed)]].set(jnp.asarray(lengths, jnp.int32))

    lengths = jnp.where(number % 4 == 0, named(crowded, number // 4), named(ordinary, number - number // 4 - 1))
    mixed = jax.random.permutation(jax.random.fold_in(own, 3), amount)
    source_of, taker = mixed[0:amount // 2 * 2:2], mixed[1:amount // 2 * 2:2]
    margin = jnp.minimum(lengths[source_of] - 1, reach - lengths[taker]) // 2
    margin = jnp.where((source_of == order[0]) | (taker == order[0]) | (lengths[taker] == 0), 0, jnp.maximum(margin, 0))
    passed = jax.random.randint(jax.random.fold_in(own, 4), (amount // 2,), 0, 1 << 20) % (margin + 1)
    lengths = lengths.at[source_of].add(-passed).at[taker].add(passed)
    members = jnp.searchsorted(jnp.cumsum(lengths), jnp.arange(rows * top), side="right").astype(jnp.int32)
    grid = members.reshape(top, rows).T
    grid = grid[jax.random.permutation(jax.random.fold_in(own, 1), rows)]
    rotation = jax.random.randint(jax.random.fold_in(own, 2), (rows, 1), 0, top)
    return jnp.take_along_axis(grid, (jnp.arange(top)[None, :] + rotation) % top, axis=1)


def load_shares(number_of, total, limit, slope, full):
    weights = [(1 << 20) // math.isqrt(rank ** slope) + 1 for rank in range(1, number_of + 1)]
    largest = limit if full else min(limit, max(-(-total // number_of), total * weights[0] // sum(weights)))
    least = 1 if total - largest >= number_of - 1 else 0
    given, rest = [largest] + [least] * (number_of - 1), total - largest - least * (number_of - 1)
    while rest > 0:
        candidates = [i for i in range(1, number_of) if given[i] < largest] or [i for i in range(1, number_of) if given[i] < limit]
        pool, left = sum([weights[i] for i in candidates]), rest
        for i in candidates:
            more = min(limit - given[i], max(1, left * weights[i] // pool), rest)
            given[i] = given[i] + more
            rest = rest - more
    return np.array(given)


def scatter_about(key, extent, spread, bound, split=(), held_as=jnp.bfloat16):
    drawn = jax.random.normal(key, extent, jnp.float32) * spread
    if len(split) > 0:
        drawn = block_levels(key, extent, split, -0.22, 0.18) * drawn
    return jnp.clip(drawn, min=-bound, max=bound).astype(held_as)


def setup_inputs(seed: int = 0) -> dict:
    splits = jax.random.split(jax.random.key(seed), 10)
    polar_field = scatter_about(splits[0], (2, ANGLES * N_APER, RANGE_BINS * N_SWATH), 1.0, 6.0, ((1, 16), (2, 8)), jnp.float32)
    tap_index = with_ends(jax.random.randint(splits[1], (SECTIONS, N_APER, 2, TAPS, ANGLES), 0, ANGLES), jax.random.fold_in(splits[1], 1), 0, ANGLES - 1).astype(jnp.int32)
    tap_weight = scatter_about(splits[2], (SECTIONS, N_APER, 2, TAPS, ANGLES), 0.25, 1.5, ((1, 16),), jnp.float32)
    range_shift = jnp.clip(jax.random.uniform(splits[3], (SECTIONS, N_APER, 2, ANGLES), jnp.float32, -8.0, 8.0) * block_levels(splits[3], (SECTIONS, N_APER, 2, ANGLES), ((1, 16),), -0.4, 0.0), -8.0, 8.0)
    range_gain = jnp.clip(1.0 + 0.18 * jax.random.normal(splits[4], (SECTIONS, RANGE_BINS * N_SWATH), jnp.float32), 0.1, 1.9)
    tile_owner_keys = jax.random.split(jax.random.fold_in(splits[5], 1), N_APER * N_SWATH * (RANGE_BINS // BLOCK_BINS) // (RANGE_BINS // BLOCK_BINS))
    tile_owner_turns = jax.random.permutation(jax.random.fold_in(splits[5], 3), N_APER * N_SWATH * (RANGE_BINS // BLOCK_BINS) // (RANGE_BINS // BLOCK_BINS))
    tile_owner = jax.vmap(lambda own, number: shared_out(jax.random.fold_in(splits[5], 2), own, number, RANGE_BINS // BLOCK_BINS, N_APER, 1, SLOTS, 2))(tile_owner_keys, tile_owner_turns).reshape((N_APER, N_SWATH, RANGE_BINS // BLOCK_BINS, 1))
    block_weights = scatter_about(splits[6], (N_APER, N_SWATH, RANGE_BINS // BLOCK_BINS, TILE_ROWS, ANGLES), ANGLES ** -0.5, 0.5, ((0, 16), (1, 8)), jnp.float32)
    kernel_index = with_ends(jax.random.randint(splits[7], (N_APER, N_SWATH), 0, KERNELS), jax.random.fold_in(splits[7], 1), 0, KERNELS - 1).astype(jnp.int32)
    kernel_bank = scatter_about(splits[8], (KERNELS, 81), 81 ** -0.5, 0.625, (), jnp.float32)
    return {"polar_field": polar_field, "tap_index": tap_index, "tap_weight": tap_weight, "range_shift": range_shift, "range_gain": range_gain, "tile_owner": tile_owner, "block_weights": block_weights, "kernel_index": kernel_index, "kernel_bank": kernel_bank}


HIGHEST_PRECISION = lax.Precision.HIGHEST


def transform_tables(length):
    bin_index = jnp.arange(length, dtype=jnp.int32)
    product = (bin_index[:, None] * bin_index[None, :]) % length
    phase_angle = product.astype(jnp.float32) * jnp.float32(2.0 * math.pi / length)
    return jnp.cos(phase_angle), jnp.sin(phase_angle)


def forward(signal, cos_table, sin_table):
    with_cos = jnp.dot(signal, cos_table, precision=HIGHEST_PRECISION, preferred_element_type=jnp.float32)
    with_sin = jnp.dot(signal, sin_table, precision=HIGHEST_PRECISION, preferred_element_type=jnp.float32)
    return jnp.stack([with_cos[0] + with_sin[1], with_cos[1] - with_sin[0]])


def inverse(signal, cos_table, sin_table):
    length = cos_table.shape[0]
    with_cos = jnp.dot(signal, cos_table, precision=HIGHEST_PRECISION, preferred_element_type=jnp.float32)
    with_sin = jnp.dot(signal, sin_table, precision=HIGHEST_PRECISION, preferred_element_type=jnp.float32)
    return jnp.stack([(with_cos[0] - with_sin[1]) / length, (with_cos[1] + with_sin[0]) / length])


def interp_matrix(tap_rows, weight_rows, length):
    columns = jnp.arange(length, dtype=jnp.int32)
    matches = (tap_rows[..., None] == columns).astype(jnp.float32)
    return jnp.sum(weight_rows[..., None] * matches, axis=-3)


def phase_tables(shift_rows, length):
    bin_index = jnp.arange(length, dtype=jnp.int32)
    signed = jnp.where(bin_index < length // 2, bin_index, bin_index - length).astype(jnp.float32)
    phase_angle = shift_rows[..., None] * signed * jnp.float32(-2.0 * math.pi / length)
    return jnp.cos(phase_angle), jnp.sin(phase_angle)


def steer_all(matrix, shift_rows, spectra):
    mixed = jnp.einsum("ikj,pijbr->pikbr", matrix.astype(jnp.float32), spectra.astype(jnp.float32), precision=HIGHEST_PRECISION)
    cos_phase, sin_phase = phase_tables(shift_rows, RANGE_BINS)
    cos_phase = cos_phase[:, :, None, :]
    sin_phase = sin_phase[:, :, None, :]
    return jnp.stack([cos_phase * mixed[0] - sin_phase * mixed[1], cos_phase * mixed[1] + sin_phase * mixed[0]])


def reference(polar_field, tap_index, tap_weight, range_shift, range_gain, tile_owner, block_weights, kernel_index, kernel_bank):
    cos_table, sin_table = transform_tables(RANGE_BINS)
    current = polar_field.reshape(2, N_APER, ANGLES, N_SWATH, RANGE_BINS)
    gain_rows = range_gain.reshape(SECTIONS, N_SWATH, RANGE_BINS)
    devices = np.arange(N_APER)
    for merge_step in range(SECTIONS):
        spectra = forward(current, cos_table, sin_table)
        matrices = interp_matrix(tap_index[merge_step], tap_weight[merge_step], ANGLES)
        lower_child = devices & ~(1 << merge_step)
        upper_child = devices | (1 << merge_step)
        merged = steer_all(matrices[:, 0], range_shift[merge_step][:, 0], spectra[:, lower_child])
        merged = merged + steer_all(matrices[:, 1], range_shift[merge_step][:, 1], spectra[:, upper_child])
        current = inverse(merged, cos_table, sin_table) * gain_rows[merge_step][None, None, None, :, :]
    blocks_dev = RANGE_BINS // BLOCK_BINS
    pieces = current.reshape(2, N_APER, ANGLES, N_SWATH, blocks_dev, BLOCK_BINS)
    contrib = jnp.einsum("asbxk,paksby->asbpxy", block_weights.astype(jnp.float32), pieces, precision=HIGHEST_PRECISION)
    owner_ids = tile_owner[..., 0]
    owner_hits = (owner_ids[..., None] == jnp.arange(N_APER, dtype=jnp.int32)).astype(jnp.float32)
    tile_grid = jnp.einsum("asbd,asbpxy->dspxy", owner_hits, contrib, precision=HIGHEST_PRECISION)
    cart_image = tile_grid.transpose(2, 0, 3, 1, 4).reshape(2, N_APER * TILE_ROWS, N_SWATH * BLOCK_BINS)
    padded = jnp.pad(cart_image, ((0, 0), (4, 4), (4, 4)))
    chosen = kernel_bank[kernel_index]
    result_sum = jnp.zeros((2, N_APER, TILE_ROWS, N_SWATH, BLOCK_BINS), jnp.float32)
    for offset in range(81):
        row_shift = offset // 9
        col_shift = offset % 9
        window = padded[:, row_shift:row_shift + N_APER * TILE_ROWS, col_shift:col_shift + N_SWATH * BLOCK_BINS]
        window = window.reshape(2, N_APER, TILE_ROWS, N_SWATH, BLOCK_BINS)
        result_sum = result_sum + chosen[:, :, offset][None, :, None, :, None] * window
    return result_sum.reshape(2, N_APER * TILE_ROWS, N_SWATH * BLOCK_BINS)
```

```python
import functools
import math

import jax
import jax.numpy as jnp
import numpy as np
from jax import lax
from jax.experimental import pallas as pl
from jax.experimental.pallas import tpu as pltpu
from jax.sharding import PartitionSpec as P

N = 1024
H = 256
A = 128
F32 = jnp.float32
BF16 = jnp.bfloat16
VMEM = pl.BlockSpec(memory_space=pltpu.VMEM)
SMEM = pl.BlockSpec(memory_space=pltpu.SMEM)


def dft_tables():
    r = np.arange(H)[:, None]
    out = []
    for m1 in range(4):
        m = 4 * np.arange(H)[None, :] + m1
        angle = 2.0 * np.pi * ((r * m) % N) / N
        c, s = np.cos(angle), np.sin(angle)
        out.append(np.stack([np.concatenate([c, s], 1), np.concatenate([c.T, s.T], 1)]))
    full = np.stack(out, 1).astype(np.float32)
    hi = full.astype(jnp.bfloat16)
    lo = (full - hi.astype(np.float32)).astype(jnp.bfloat16)
    return hi, lo


def split(x):
    hi = x.astype(BF16)
    return hi, (x - hi.astype(F32)).astype(BF16)


def dot(a, b):
    return jnp.dot(a, b, preferred_element_type=F32)


def quarter_turns(re, im, sign):
    ar, ai = re[0] + re[2], im[0] + im[2]
    br, bi = re[0] - re[2], im[0] - im[2]
    cr, ci = re[1] + re[3], im[1] + im[3]
    dr, di = re[1] - re[3], im[1] - im[3]
    if sign > 0:
        er, ei = -di, dr
    else:
        er, ei = di, -dr
    return [ar + cr, br + er, ar - cr, br - er], [ai + ci, bi + ei, ai - ci, bi - ei]


def sincos_turns(t):
    t = t - jnp.round(t)
    q = jnp.round(t * 4.0)
    y = (t - q * 0.25) * F32(2.0 * math.pi)
    y2 = y * y
    s = y * (1.0 + y2 * (-1.0 / 6 + y2 * (1.0 / 120 + y2 * (-1.0 / 5040 + y2 * (1.0 / 362880)))))
    c = 1.0 + y2 * (-0.5 + y2 * (1.0 / 24 + y2 * (-1.0 / 720 + y2 * (1.0 / 40320 - y2 * (1.0 / 3628800)))))
    odd = jnp.abs(q) == 1.0
    half = jnp.abs(q) == 2.0
    sign = jnp.where(q < 0, -1.0, 1.0)
    cc = jnp.where(odd, -sign * s, jnp.where(half, -c, c))
    ss = jnp.where(odd, sign * c, jnp.where(half, -s, s))
    return cc, ss


def prepare(tab, at, mats, phases, steps):
    rows = lax.broadcasted_iota(jnp.int32, (A, A), 0).astype(F32)
    total = jnp.zeros((A, A), F32)
    for t in range(8):
        total = total + jnp.where(rows == tab[t : t + 1, :], tab[8 + t : 9 + t, :], 0.0)
    hi, lo = split(total.T)
    mats[at, 0:A, 0:A] = hi
    mats[at, 0:A, A:] = hi
    mats[at, A:, 0:A] = lo
    mats[at, A:, A:] = jnp.zeros((A, A), BF16)
    shift = jnp.broadcast_to(tab[16:17, :], (A, A)).T
    lane = lax.broadcasted_iota(jnp.int32, (A, A), 1).astype(F32)
    c, s = sincos_turns(shift * lane * F32(-4.0 / N))
    hc, hs = sincos_turns(shift * F32(0.5))
    phases[at, 0, :, 0:A] = c
    phases[at, 1, :, 0:A] = s
    phases[at, 0, :, A:] = c * hc - s * hs
    phases[at, 1, :, A:] = c * hs + s * hc
    c1, s1 = sincos_turns(shift * F32(-1.0 / N))
    steps[at, 0] = c1
    steps[at, 1] = s1


def put_split(ref, m1, signals, n, which, re, im):
    rh, rl = split(re)
    ih, il = split(im)
    for part, value in enumerate((rh, ih, rl, il)):
        base = (part // 2) * 2 * n * A + (part % 2) * n * A + which * A
        ref[m1, base : base + A, :] = value


def product(lhs, hi, lo, rows):
    both = dot(lhs, hi)
    return both[:rows] + both[rows:] + dot(lhs[:rows], lo)


def stage(inputs, plan, zz, uu, hi_ref, lo_ref, mats, phases, steps):
    n_in, n_out = len(inputs), len(plan)
    for which, (re, im) in enumerate(inputs):
        zr, zi = quarter_turns(re, im, -1)
        for m1 in range(4):
            put_split(zz, m1, None, n_in, which, zr[m1], zi[m1])

    def body(m1, carry):
        rows = 2 * n_in * A
        p = product(zz[m1, : 2 * rows, :], hi_ref[0, m1], lo_ref[0, m1], rows)
        half = n_in * A
        xr = p[:half, :H] + p[half:, H:]
        xi = p[half:, :H] - p[:half, H:]
        stacked = []
        for which in range(n_in):
            x = jnp.concatenate([xr[which * A : which * A + A], xi[which * A : which * A + A]], axis=1)
            h, l = split(x)
            stacked.append(jnp.concatenate([h, l], axis=0))
        parts = [[], [], [], []]
        for terms in plan:
            mr = mi = None
            for which, at in terms:
                y = dot(mats[at], stacked[which])
                y = y[:A] + y[A:]
                yr, yi = y[:, :H], y[:, H:]
                c, s = phases[at, 0], phases[at, 1]
                tr, ti = c * yr - s * yi, c * yi + s * yr
                mr, mi = (tr, ti) if mr is None else (mr + tr, mi + ti)
                c1, s1 = steps[at, 0], steps[at, 1]
                c1 = jnp.concatenate([c1, c1], axis=1)
                s1 = jnp.concatenate([s1, s1], axis=1)
                phases[at, 0] = c * c1 - s * s1
                phases[at, 1] = c * s1 + s * c1
            rh, rl = split(mr)
            ih, il = split(mi)
            for k, v in enumerate((rh, ih, rl, il)):
                parts[k].append(v)
        lhs = jnp.concatenate([v for part in parts for v in part], axis=0)
        rows = 2 * n_out * A
        p = product(lhs, hi_ref[1, m1], lo_ref[1, m1], rows)
        half = n_out * A
        uu[m1, :half, :H] = p[:half, :H] - p[half:, H:]
        uu[m1, :half, H:] = p[:half, H:] + p[half:, :H]
        return carry

    lax.fori_loop(0, 4, body, 0)
    out = []
    for which in range(n_out):
        base = which * A
        re = [uu[m1, base : base + A, :H] for m1 in range(4)]
        im = [uu[m1, base : base + A, H:] for m1 in range(4)]
        out.append(quarter_turns(re, im, 1))
    return out


def gained(blocks, gain, section):
    re, im = blocks
    rows = [gain[section : section + 1, H * k : H * k + H] * F32(1.0 / N) for k in range(4)]
    return [v * g for v, g in zip(re, rows)], [v * g for v, g in zip(im, rows)]


def merge_kernel(bits, own, other, tab, tabx, taby, tabd, gain, hi, lo, out, zz, uu, mats, phases, steps):
    b0, b1, b2 = bits[0], bits[1], bits[2]
    prepare(tab[b0], 0, mats, phases, steps)
    prepare(tab[1 - b0], 1, mats, phases, steps)
    prepare(tab[2 + b1], 2, mats, phases, steps)
    prepare(tabx[2 + b1], 3, mats, phases, steps)
    for at, ref in ((4, tab), (5, tabx), (6, taby), (7, tabd)):
        prepare(ref[4 + b2], at, mats, phases, steps)
    run = functools.partial(stage, zz=zz, uu=uu, hi_ref=hi, lo_ref=lo, mats=mats, phases=phases, steps=steps)

    def blocks(ref):
        return [[ref[p, :, H * k : H * k + H] for k in range(4)] for p in range(2)]

    first = run([blocks(own), blocks(other)], [[(0, 0), (1, 1)]])
    y = gained(first[0], gain, 0)
    second = run([y], [[(0, 2)], [(0, 3)]])
    z = [gained(v, gain, 1) for v in second]
    third = run(z, [[(0, 4)], [(1, 5)], [(0, 6)], [(1, 7)]])
    for j, v in enumerate(third):
        re, im = gained(v, gain, 2)
        for k in range(4):
            for part in range(2):
                both = jnp.concatenate(
                    [re[k][:, A * part : A * part + A], im[k][:, A * part : A * part + A]], axis=1
                )
                h, l = split(both)
                out[j, 2 * k + part, 0:A] = h
                out[j, 2 * k + part, A:] = l


ROWS = A + 8


def contrib_kernel(owners, bits, cur, w0, w1, w2, w3, keep, send, acc):
    acc[...] = jnp.zeros_like(acc)
    row = lax.broadcasted_iota(jnp.int32, (8, H), 0)

    def place(owner):
        return (owner % 2) * 8 + owner // 2

    for j, w in enumerate((w0, w1, w2, w3)):

        def body(q, carry):
            h, l = split(w[q])
            x = cur[j, q]
            c = dot(h, x[:A]) + dot(l, x[:A]) + dot(h, x[A:])
            owner = owners[j * 8 + q]
            acc[place(owner), 0:A] += c
            top = pltpu.roll(c[A - 8 :], 4, 0)
            bottom = pltpu.roll(c[:8], 4, 0)

            @pl.when(owner < 15)
            def _():
                acc[place(owner + 1), A:] += jnp.where(row < 4, top, 0.0)

            @pl.when(owner > 0)
            def _():
                acc[place(owner - 1), A:] += jnp.where(row >= 4, bottom, 0.0)

            return carry

        lax.fori_loop(0, 8, body, 0)
    mine = pl.multiple_of(bits[0] * 8, 8)
    theirs = pl.multiple_of(8 - bits[0] * 8, 8)
    keep[...] = acc[pl.ds(mine, 8)]
    send[...] = acc[pl.ds(theirs, 8)]


def add_kernel(a, b, out):
    out[...] = a[...] + b[...]


def tile_kernel(parts, tile, first, last):
    total = parts[0]
    for k in range(1, 8):
        total = total + parts[k]
    tile[...] = total
    first[...] = jnp.concatenate([total[:, 0:A], total[:, A:]], axis=0)
    last[...] = jnp.concatenate([total[:, 0:A], total[:, A:]], axis=0)


def filter_kernel(index, bank, tile, before, after, out, pad, moved):
    number = index[0, 0]
    for p in range(2):
        body = tile[:, A * p : A * p + A]
        lead = before[ROWS * p : ROWS * p + ROWS, :]
        tail = after[ROWS * p : ROWS * p + ROWS, :]
        lane = lax.broadcasted_iota(jnp.int32, (ROWS, A), 1)
        turned = pltpu.roll(body, 4, 1)
        left = jnp.where(lane < 4, pltpu.roll(lead, 4, 1), turned)
        right = jnp.where(lane < 4, turned, pltpu.roll(tail, 4, 1))
        for half, value in enumerate((left, right)):
            pad[4 : 4 + A, A * half : A * half + A] = value[0:A]
            pad[0:4, A * half : A * half + A] = value[A : A + 4]
            pad[A + 4 :, A * half : A * half + A] = value[A + 4 :]
        total = jnp.zeros((A, A), F32)
        for v in range(9):
            if v:
                moved[...] = pltpu.roll(pad[...], H - v, 1)[:, :A]
            else:
                moved[...] = pad[:, :A]
            for u in range(9):
                total = total + bank[number, 9 * u + v] * moved[u : u + A, :]
        out[p] = total


def call(kernel, out_shape, in_specs, scratch=(), flops=1000000):
    return pl.pallas_call(
        kernel,
        out_shape=out_shape,
        in_specs=in_specs,
        out_specs=jax.tree.map(lambda _: VMEM, out_shape),
        scratch_shapes=list(scratch),
        compiler_params=pltpu.CompilerParams(vmem_limit_bytes=48 << 20),
        cost_estimate=pl.CostEstimate(flops=flops, bytes_accessed=1 << 20, transcendentals=0),
    )


def struct(shape, dtype=F32):
    return jax.ShapeDtypeStruct(shape, dtype)


def swap(value, mask):
    return lax.ppermute(value, "aper", [(i, i ^ mask) for i in range(16)])


def shards(polar, tap_index, tap_weight, range_shift, range_gain, tile_owner, weights, kernel_index, bank):
    place = lax.axis_index("aper")
    bits = jnp.stack([place % 2, place // 2 % 2, place // 4 % 2]).astype(jnp.int32)
    owner_row = jnp.zeros((8, A), F32).at[:, 0:8].set(tile_owner[0, 0, :, 0].astype(F32)[None, :])
    tab = jnp.concatenate(
        [
            tap_index[:, 0].astype(F32),
            tap_weight[:, 0],
            jnp.broadcast_to(range_shift[:, 0, :, None, :], (3, 2, 4, A)),
            jnp.broadcast_to(owner_row[0:4], (3, 2, 4, A)),
        ],
        axis=2,
    ).reshape(6, 24, A)
    tabx, taby, tabd = (swap(tab, mask) for mask in (2, 4, 6))
    other = swap(polar, 1)
    own_weights = weights[0, 0]
    wx, wy, wd = (swap(own_weights, mask) for mask in (2, 4, 6))
    hi, lo = dft_tables()
    cur = call(
        merge_kernel,
        struct((4, 8, 2 * A, H), BF16),
        [SMEM] + [VMEM] * 9,
        [
            pltpu.VMEM((4, 8 * A, H), BF16),
            pltpu.VMEM((4, 4 * A, 2 * H), F32),
            pltpu.VMEM((8, 2 * A, 2 * A), BF16),
            pltpu.VMEM((8, 2, A, H), F32),
            pltpu.VMEM((8, 2, A, A), F32),
        ],
        flops=12 * 10**9,
    )(bits, polar, other, tab, tabx, taby, tabd, range_gain, jnp.asarray(hi), jnp.asarray(lo))
    owners = jnp.concatenate([t[0, 20, 0:8] for t in (tab, tabx, taby, tabd)]).astype(jnp.int32)
    keep, send = call(
        contrib_kernel,
        (struct((8, ROWS, H)), struct((8, ROWS, H))),
        [SMEM, SMEM] + [VMEM] * 5,
        [pltpu.VMEM((16, ROWS, H), F32)],
        flops=10**9,
    )(owners, bits, cur, own_weights, wx, wy, wd)
    taken = swap(send, 1)
    half = keep + taken
    groups = [[c + 2 * k for k in range(8)] for c in range(2)]
    parts = lax.all_to_all(half, "aper", split_axis=0, concat_axis=0, axis_index_groups=groups, tiled=True)
    tile, first, last = call(
        tile_kernel, (struct((ROWS, H)), struct((2 * ROWS, A)), struct((2 * ROWS, A))), [VMEM]
    )(parts)
    before = lax.ppermute(last, "swath", [(i, i + 1) for i in range(7)])
    after = lax.ppermute(first, "swath", [(i + 1, i) for i in range(7)])
    return call(
        filter_kernel,
        struct((2, A, A)),
        [SMEM, SMEM] + [VMEM] * 3,
        [pltpu.VMEM((ROWS, H), F32), pltpu.VMEM((ROWS, A), F32)],
    )(kernel_index, bank, tile, before, after)


def solution(mesh):
    in_specs = (
        P(None, "aper", "swath"),
        P(None, "aper", None, None, None),
        P(None, "aper", None, None, None),
        P(None, "aper", None, None),
        P(None, "swath"),
        P("aper", "swath", None, None),
        P("aper", "swath", None, None, None),
        P("aper", "swath"),
        P(),
    )
    out_specs = P(None, "aper", "swath")
    return jax.shard_map(shards, mesh=mesh, in_specs=in_specs, out_specs=out_specs, check_vma=False)
```

```python
import functools
import math

import jax
import jax.numpy as jnp
import numpy as np
from jax import lax
from jax.experimental import pallas as pl
from jax.experimental.pallas import tpu as pltpu
from jax.sharding import PartitionSpec as P

N = 1024
H = 256
A = 128
F32 = jnp.float32
BF16 = jnp.bfloat16
VMEM = pl.BlockSpec(memory_space=pltpu.VMEM)
SMEM = pl.BlockSpec(memory_space=pltpu.SMEM)


def dft_tables():
    r = np.arange(A)[:, None]
    out = []
    for m1 in range(8):
        m = 8 * np.arange(A)[None, :] + m1
        angle = 2.0 * np.pi * ((r * m) % N) / N
        c, s = np.cos(angle), np.sin(angle)
        forward = np.block([[c, -s], [s, c]])
        out.append(np.stack([forward, forward.T]))
    full = np.stack(out, 1).astype(np.float32)
    hi = full.astype(jnp.bfloat16)
    lo = (full - hi.astype(np.float32)).astype(jnp.bfloat16)
    return hi, lo


def split(x):
    hi = x.astype(BF16)
    return hi, (x - hi.astype(F32)).astype(BF16)


def dot(a, b):
    return jnp.dot(a, b, preferred_element_type=F32)


def quarter_turns(re, im, sign):
    ar, ai = re[0] + re[2], im[0] + im[2]
    br, bi = re[0] - re[2], im[0] - im[2]
    cr, ci = re[1] + re[3], im[1] + im[3]
    dr, di = re[1] - re[3], im[1] - im[3]
    if sign > 0:
        er, ei = -di, dr
    else:
        er, ei = di, -dr
    return [ar + cr, br + er, ar - cr, br - er], [ai + ci, bi + ei, ai - ci, bi - ei]


def eighth_turns(re, im, sign):
    er, ei = quarter_turns(re[0::2], im[0::2], sign)
    br, bi = quarter_turns(re[1::2], im[1::2], sign)
    root = F32(math.sqrt(0.5))
    if sign > 0:
        tr = [br[0], (br[1] - bi[1]) * root, -bi[2], (br[3] + bi[3]) * -root]
        ti = [bi[0], (bi[1] + br[1]) * root, br[2], (br[3] - bi[3]) * root]
    else:
        tr = [br[0], (br[1] + bi[1]) * root, bi[2], (bi[3] - br[3]) * root]
        ti = [bi[0], (bi[1] - br[1]) * root, -br[2], (bi[3] + br[3]) * -root]
    out_re = [e + t for e, t in zip(er, tr)] + [e - t for e, t in zip(er, tr)]
    out_im = [e + t for e, t in zip(ei, ti)] + [e - t for e, t in zip(ei, ti)]
    return out_re, out_im


def sincos_turns(t):
    t = t - jnp.round(t)
    q = jnp.round(t * 4.0)
    y = (t - q * 0.25) * F32(2.0 * math.pi)
    y2 = y * y
    s = y * (1.0 + y2 * (-1.0 / 6 + y2 * (1.0 / 120 + y2 * (-1.0 / 5040 + y2 * (1.0 / 362880)))))
    c = 1.0 + y2 * (-0.5 + y2 * (1.0 / 24 + y2 * (-1.0 / 720 + y2 * (1.0 / 40320 - y2 * (1.0 / 3628800)))))
    odd = jnp.abs(q) == 1.0
    half = jnp.abs(q) == 2.0
    sign = jnp.where(q < 0, -1.0, 1.0)
    cc = jnp.where(odd, -sign * s, jnp.where(half, -c, c))
    ss = jnp.where(odd, sign * c, jnp.where(half, -s, s))
    return cc, ss


def prepare(tab, at, mats, phases, steps):
    rows = lax.broadcasted_iota(jnp.int32, (A, A), 0).astype(F32)
    total = jnp.zeros((A, A), F32)
    for t in range(8):
        total = total + jnp.where(rows == tab[t : t + 1, :], tab[8 + t : 9 + t, :], 0.0)
    hi, lo = split(total.T)
    mats[at, 0:A, 0:A] = hi
    mats[at, 0:A, A:] = hi
    mats[at, A:, 0:A] = lo
    mats[at, A:, A:] = jnp.zeros((A, A), BF16)
    shift = jnp.broadcast_to(tab[16:17, :], (A, A)).T
    lane = lax.broadcasted_iota(jnp.int32, (A, A), 1)
    lane = jnp.where(lane < A // 2, lane, lane - A).astype(F32)
    c, s = sincos_turns(shift * lane * F32(-8.0 / N))
    phases[at, 0] = c
    phases[at, 1] = s
    c1, s1 = sincos_turns(shift * F32(-1.0 / N))
    steps[at, 0] = c1
    steps[at, 1] = s1


def product(lhs, hi, lo, rows):
    both = dot(lhs, hi)
    return both[:rows] + both[rows:] + dot(lhs[:rows], lo)


def stage(inputs, plan, zz, uu, hi_ref, lo_ref, mats, phases, steps):
    n_in, n_out = len(inputs), len(plan)
    rows_in, rows_out = n_in * A, n_out * A
    for which, (re, im) in enumerate(inputs):
        zr, zi = eighth_turns(re, im, -1)
        for m1 in range(8):
            h, l = split(jnp.concatenate([zr[m1], zi[m1]], axis=1))
            zz[m1, which * A : which * A + A] = h
            zz[m1, rows_in + which * A : rows_in + which * A + A] = l
    turns = {at: (phases[at, 0], phases[at, 1]) for terms in plan for _, at in terms}
    for m1 in range(8):
        x = product(zz[m1, : 2 * rows_in], hi_ref[0, m1], lo_ref[0, m1], rows_in)
        h, l = split(x)
        stacked = [
            jnp.concatenate([h[which * A : which * A + A], l[which * A : which * A + A]], axis=0)
            for which in range(n_in)
        ]
        highs, lows = [], []
        for terms in plan:
            mr = mi = None
            for which, at in terms:
                y = dot(mats[at], stacked[which])
                y = y[:A] + y[A:]
                yr, yi = y[:, :A], y[:, A:]
                c, s = turns[at]
                tr, ti = c * yr - s * yi, c * yi + s * yr
                mr, mi = (tr, ti) if mr is None else (mr + tr, mi + ti)
                if m1 < 7:
                    c1, s1 = steps[at, 0], steps[at, 1]
                    turns[at] = (c * c1 - s * s1, c * s1 + s * c1)
            h, l = split(jnp.concatenate([mr, mi], axis=1))
            highs.append(h)
            lows.append(l)
        lhs = jnp.concatenate(highs + lows, axis=0)
        uu[m1, :rows_out] = product(lhs, hi_ref[1, m1], lo_ref[1, m1], rows_out)
    out = []
    for which in range(n_out):
        base = which * A
        re = [uu[m1, base : base + A, :A] for m1 in range(8)]
        im = [uu[m1, base : base + A, A:] for m1 in range(8)]
        out.append(eighth_turns(re, im, 1))
    return out


def gained(blocks, gain, section):
    re, im = blocks
    rows = [gain[section : section + 1, A * k : A * k + A] * F32(1.0 / N) for k in range(8)]
    return [v * g for v, g in zip(re, rows)], [v * g for v, g in zip(im, rows)]


def merge_kernel(bits, own, other, tab, tabx, taby, tabd, gain, hi, lo, out, zz, uu, mats, phases, steps):
    b0, b1, b2 = bits[0], bits[1], bits[2]
    prepare(tab[b0], 0, mats, phases, steps)
    prepare(tab[1 - b0], 1, mats, phases, steps)
    prepare(tab[2 + b1], 2, mats, phases, steps)
    prepare(tabx[2 + b1], 3, mats, phases, steps)
    for at, ref in ((4, tab), (5, tabx), (6, taby), (7, tabd)):
        prepare(ref[4 + b2], at, mats, phases, steps)
    run = functools.partial(stage, zz=zz, uu=uu, hi_ref=hi, lo_ref=lo, mats=mats, phases=phases, steps=steps)

    def blocks(ref):
        return [[ref[p, :, A * k : A * k + A] for k in range(8)] for p in range(2)]

    first = run([blocks(own), blocks(other)], [[(0, 0), (1, 1)]])
    y = gained(first[0], gain, 0)
    second = run([y], [[(0, 2)], [(0, 3)]])
    z = [gained(v, gain, 1) for v in second]
    third = run(z, [[(0, 4)], [(1, 5)], [(0, 6)], [(1, 7)]])
    for j, v in enumerate(third):
        re, im = gained(v, gain, 2)
        for q in range(8):
            h, l = split(jnp.concatenate([re[q], im[q]], axis=1))
            out[j, q, 0:A] = h
            out[j, q, A:] = l


ROWS = A + 8


def contrib_kernel(owners, bits, cur, w0, w1, w2, w3, keep, send, acc):
    acc[...] = jnp.zeros_like(acc)
    row = lax.broadcasted_iota(jnp.int32, (8, H), 0)

    def place(owner):
        return (owner % 2) * 8 + owner // 2

    for j, w in enumerate((w0, w1, w2, w3)):
        for q in range(8):
            h, l = split(w[q])
            x = cur[j, q]
            c = dot(jnp.concatenate([h, h], axis=1), x) + dot(l, x[:A])
            owner = owners[j * 8 + q]
            acc[place(owner), 0:A] += c
            top = pltpu.roll(c[A - 8 :], 4, 0)
            bottom = pltpu.roll(c[:8], 4, 0)
            above = jnp.maximum(owner - 1, 0)
            below = jnp.minimum(owner + 1, 15)
            acc[place(below), A:] += jnp.where((row < 4) & (owner < 15), top, 0.0)
            acc[place(above), A:] += jnp.where((row >= 4) & (owner > 0), bottom, 0.0)
    mine = pl.multiple_of(bits[0] * 8, 8)
    theirs = pl.multiple_of(8 - bits[0] * 8, 8)
    keep[...] = acc[pl.ds(mine, 8)]
    send[...] = acc[pl.ds(theirs, 8)]


def add_kernel(a, b, out):
    out[...] = a[...] + b[...]


def tile_kernel(parts, tile, first, last):
    total = parts[0]
    for k in range(1, 8):
        total = total + parts[k]
    tile[...] = total
    re, im = total[:, :A], total[:, A:]
    lane = lax.broadcasted_iota(jnp.int32, (ROWS, A), 1)
    for ref, edge in (
        (first, jnp.where(lane < 4, re, pltpu.roll(im, 4, 1))),
        (last, jnp.where(lane < 4, pltpu.roll(re, 4, 1), pltpu.roll(im, 8, 1))),
    ):
        ref[:, :A] = edge[:A].T[:8]
        ends = jnp.concatenate([edge[A:], jnp.zeros((A - 8, A), F32)], axis=0)
        ref[:, A:] = ends.T[:8]


def filter_kernel(index, bank, tile, before, after, out, pad, moved):
    number = index[0, 0]
    sides = []
    for ref in (before, after):
        blank = jnp.zeros((A - 8, A), F32)
        main = jnp.concatenate([ref[:, :A], blank], axis=0).T
        ends = jnp.concatenate([ref[:, A:], blank], axis=0).T
        sides.append(jnp.concatenate([main, ends[:8]], axis=0))
    lane = lax.broadcasted_iota(jnp.int32, (ROWS, A), 1)
    for p in range(2):
        body = tile[:, A * p : A * p + A]
        turned = pltpu.roll(body, 4, 1)
        lead = sides[0] if p == 0 else pltpu.roll(sides[0], A - 4, 1)
        tail = pltpu.roll(sides[1], 4, 1) if p == 0 else sides[1]
        left = jnp.where(lane < 4, lead, turned)
        right = jnp.where(lane < 4, turned, tail)
        for half, value in enumerate((left, right)):
            pad[4 : 4 + A, A * half : A * half + A] = value[0:A]
            pad[0:4, A * half : A * half + A] = value[A : A + 4]
            pad[A + 4 :, A * half : A * half + A] = value[A + 4 :]
        total = jnp.zeros((A, A), F32)
        for v in range(9):
            if v:
                moved[...] = pltpu.roll(pad[...], H - v, 1)[:, :A]
            else:
                moved[...] = pad[:, :A]
            for u in range(9):
                total = total + bank[number, 9 * u + v] * moved[u : u + A, :]
        out[p] = total


def call(kernel, out_shape, in_specs, scratch=(), flops=1000000):
    return pl.pallas_call(
        kernel,
        out_shape=out_shape,
        in_specs=in_specs,
        out_specs=jax.tree.map(lambda _: VMEM, out_shape),
        scratch_shapes=list(scratch),
        compiler_params=pltpu.CompilerParams(vmem_limit_bytes=48 << 20),
        cost_estimate=pl.CostEstimate(flops=flops, bytes_accessed=1 << 20, transcendentals=0),
    )


def struct(shape, dtype=F32):
    return jax.ShapeDtypeStruct(shape, dtype)


def swap(value, mask):
    return lax.ppermute(value, "aper", [(i, i ^ mask) for i in range(16)])


def shards(polar, tap_index, tap_weight, range_shift, range_gain, tile_owner, weights, kernel_index, bank):
    place = lax.axis_index("aper")
    bits = jnp.stack([place % 2, place // 2 % 2, place // 4 % 2]).astype(jnp.int32)
    owner_row = jnp.zeros((8, A), F32).at[:, 0:8].set(tile_owner[0, 0, :, 0].astype(F32)[None, :])
    tab = jnp.concatenate(
        [
            tap_index[:, 0].astype(F32),
            tap_weight[:, 0],
            jnp.broadcast_to(range_shift[:, 0, :, None, :], (3, 2, 4, A)),
            jnp.broadcast_to(owner_row[0:4], (3, 2, 4, A)),
        ],
        axis=2,
    ).reshape(6, 24, A)
    tabx, taby, tabd = (swap(tab, mask) for mask in (2, 4, 6))
    other = swap(polar, 1)
    own_weights = weights[0, 0]
    wx, wy, wd = (swap(own_weights, mask) for mask in (2, 4, 6))
    hi, lo = dft_tables()
    cur = call(
        merge_kernel,
        struct((4, 8, 2 * A, H), BF16),
        [SMEM] + [VMEM] * 9,
        [
            pltpu.VMEM((8, 4 * A, H), BF16),
            pltpu.VMEM((8, 4 * A, H), F32),
            pltpu.VMEM((8, 2 * A, 2 * A), BF16),
            pltpu.VMEM((8, 2, A, A), F32),
            pltpu.VMEM((8, 2, A, A), F32),
        ],
        flops=12 * 10**9,
    )(bits, polar, other, tab, tabx, taby, tabd, range_gain, jnp.asarray(hi), jnp.asarray(lo))
    owners = jnp.concatenate([t[0, 20, 0:8] for t in (tab, tabx, taby, tabd)]).astype(jnp.int32)
    keep, send = call(
        contrib_kernel,
        (struct((8, ROWS, H)), struct((8, ROWS, H))),
        [SMEM, SMEM] + [VMEM] * 5,
        [pltpu.VMEM((16, ROWS, H), F32)],
        flops=10**9,
    )(owners, bits, cur, own_weights, wx, wy, wd)
    taken = swap(send, 1)
    half = keep + taken
    groups = [[c + 2 * k for k in range(8)] for c in range(2)]
    parts = lax.all_to_all(half, "aper", split_axis=0, concat_axis=0, axis_index_groups=groups, tiled=True)
    tile, first, last = call(
        tile_kernel, (struct((ROWS, H)), struct((8, H)), struct((8, H))), [VMEM]
    )(parts)
    before = lax.ppermute(last, "swath", [(i, i + 1) for i in range(7)])
    after = lax.ppermute(first, "swath", [(i + 1, i) for i in range(7)])
    return call(
        filter_kernel,
        struct((2, A, A)),
        [SMEM, SMEM] + [VMEM] * 3,
        [pltpu.VMEM((ROWS, H), F32), pltpu.VMEM((ROWS, A), F32)],
    )(kernel_index, bank, tile, before, after)


def solution(mesh):
    in_specs = (
        P(None, "aper", "swath"),
        P(None, "aper", None, None, None),
        P(None, "aper", None, None, None),
        P(None, "aper", None, None),
        P(None, "swath"),
        P("aper", "swath", None, None),
        P("aper", "swath", None, None, None),
        P("aper", "swath"),
        P(),
    )
    out_specs = P(None, "aper", "swath")
    return jax.shard_map(shards, mesh=mesh, in_specs=in_specs, out_specs=out_specs, check_vma=False)
```

```python
import functools
import math

import jax
import jax.numpy as jnp
import numpy as np
from jax import lax
from jax.experimental import pallas as pl
from jax.experimental.pallas import tpu as pltpu
from jax.sharding import PartitionSpec as P

N = 1024
H = 256
A = 128
F32 = jnp.float32
BF16 = jnp.bfloat16
VMEM = pl.BlockSpec(memory_space=pltpu.VMEM)
HBM = pl.BlockSpec(memory_space=pltpu.HBM)
SMEM = pl.BlockSpec(memory_space=pltpu.SMEM)


def dft_tables():
    r = np.arange(A)[:, None]
    out = []
    for m1 in range(8):
        m = 8 * np.arange(A)[None, :] + m1
        angle = 2.0 * np.pi * ((r * m) % N) / N
        c, s = np.cos(angle), np.sin(angle)
        forward = np.block([[c, -s], [s, c]])
        out.append(forward)
    full = np.stack(out).astype(np.float32)
    hi = full.astype(jnp.bfloat16)
    lo = (full - hi.astype(np.float32)).astype(jnp.bfloat16)
    return np.stack([hi, lo])


def split(x):
    hi = x.astype(BF16)
    return hi, (x - hi.astype(F32)).astype(BF16)


def dot(a, b):
    return jnp.dot(a, b, preferred_element_type=F32)


def quarter_turns(re, im, sign):
    ar, ai = re[0] + re[2], im[0] + im[2]
    br, bi = re[0] - re[2], im[0] - im[2]
    cr, ci = re[1] + re[3], im[1] + im[3]
    dr, di = re[1] - re[3], im[1] - im[3]
    if sign > 0:
        er, ei = -di, dr
    else:
        er, ei = di, -dr
    return [ar + cr, br + er, ar - cr, br - er], [ai + ci, bi + ei, ai - ci, bi - ei]


def eighth_turns(re, im, sign):
    er, ei = quarter_turns(re[0::2], im[0::2], sign)
    br, bi = quarter_turns(re[1::2], im[1::2], sign)
    root = F32(math.sqrt(0.5))
    if sign > 0:
        tr = [br[0], (br[1] - bi[1]) * root, -bi[2], (br[3] + bi[3]) * -root]
        ti = [bi[0], (bi[1] + br[1]) * root, br[2], (br[3] - bi[3]) * root]
    else:
        tr = [br[0], (br[1] + bi[1]) * root, bi[2], (bi[3] - br[3]) * root]
        ti = [bi[0], (bi[1] - br[1]) * root, -br[2], (bi[3] + br[3]) * -root]
    out_re = [e + t for e, t in zip(er, tr)] + [e - t for e, t in zip(er, tr)]
    out_im = [e + t for e, t in zip(ei, ti)] + [e - t for e, t in zip(ei, ti)]
    return out_re, out_im


def sincos_turns(t):
    t = t - jnp.round(t)
    q = jnp.round(t * 4.0)
    y = (t - q * 0.25) * F32(2.0 * math.pi)
    y2 = y * y
    s = y * (1.0 + y2 * (-1.0 / 6 + y2 * (1.0 / 120 + y2 * (-1.0 / 5040 + y2 * (1.0 / 362880)))))
    c = 1.0 + y2 * (-0.5 + y2 * (1.0 / 24 + y2 * (-1.0 / 720 + y2 * (1.0 / 40320 - y2 * (1.0 / 3628800)))))
    odd = jnp.abs(q) == 1.0
    half = jnp.abs(q) == 2.0
    sign = jnp.where(q < 0, -1.0, 1.0)
    cc = jnp.where(odd, -sign * s, jnp.where(half, -c, c))
    ss = jnp.where(odd, sign * c, jnp.where(half, -s, s))
    return cc, ss


def prepare(tab, at, mats, phases, steps):
    rows = lax.broadcasted_iota(jnp.int32, (A, A), 0).astype(F32)
    total = jnp.zeros((A, A), F32)
    for t in range(8):
        total = total + jnp.where(rows == tab[t : t + 1, :], tab[8 + t : 9 + t, :], 0.0)
    hi, lo = split(total.T)
    mats[at, 0:A, 0:A] = hi
    mats[at, 0:A, A:] = hi
    mats[at, A:, 0:A] = lo
    mats[at, A:, A:] = jnp.zeros((A, A), BF16)
    shift = jnp.broadcast_to(tab[16:17, :], (A, A)).T
    lane = lax.broadcasted_iota(jnp.int32, (A, A), 1)
    lane = jnp.where(lane < A // 2, lane, lane - A).astype(F32)
    c, s = sincos_turns(shift * lane * F32(-8.0 / N))
    phases[at, 0] = c
    phases[at, 1] = s
    c1, s1 = sincos_turns(shift * F32(-1.0 / N))
    steps[at, 0] = c1
    steps[at, 1] = s1


def product(lhs, table, m1, rows, dims):
    def by(a, b):
        return lax.dot_general(a, b, (dims, ((), ())), preferred_element_type=F32)

    both = by(lhs, table[0, m1])
    return both[:rows] + both[rows:] + by(lhs[:rows], table[1, m1])


def stage(inputs, plan, zz, uu, table, mats, phases, steps):
    n_in, n_out = len(inputs), len(plan)
    rows_in, rows_out = n_in * A, n_out * A
    for which, (re, im) in enumerate(inputs):
        zr, zi = eighth_turns(re, im, -1)
        for m1 in range(8):
            h, l = split(jnp.concatenate([zr[m1], zi[m1]], axis=1))
            zz[m1, which * A : which * A + A] = h
            zz[m1, rows_in + which * A : rows_in + which * A + A] = l
    turns = {at: (phases[at, 0], phases[at, 1]) for terms in plan for _, at in terms}
    for m1 in range(8):
        x = product(zz[m1, : 2 * rows_in], table, m1, rows_in, ((1,), (0,)))
        h, l = split(x)
        stacked = [
            jnp.concatenate([h[which * A : which * A + A], l[which * A : which * A + A]], axis=0)
            for which in range(n_in)
        ]
        highs, lows = [], []
        for terms in plan:
            mr = mi = None
            for which, at in terms:
                y = dot(mats[at], stacked[which])
                y = y[:A] + y[A:]
                yr, yi = y[:, :A], y[:, A:]
                c, s = turns[at]
                tr, ti = c * yr - s * yi, c * yi + s * yr
                mr, mi = (tr, ti) if mr is None else (mr + tr, mi + ti)
                if m1 < 7:
                    c1, s1 = steps[at, 0], steps[at, 1]
                    turns[at] = (c * c1 - s * s1, c * s1 + s * c1)
            h, l = split(jnp.concatenate([mr, mi], axis=1))
            highs.append(h)
            lows.append(l)
        lhs = jnp.concatenate(highs + lows, axis=0)
        uu[m1, :rows_out] = product(lhs, table, m1, rows_out, ((1,), (1,)))
    out = []
    for which in range(n_out):
        base = which * A
        re = [uu[m1, base : base + A, :A] for m1 in range(8)]
        im = [uu[m1, base : base + A, A:] for m1 in range(8)]
        out.append(eighth_turns(re, im, 1))
    return out


def gained(blocks, gain, section):
    re, im = blocks
    rows = [gain[section : section + 1, A * k : A * k + A] * F32(1.0 / N) for k in range(8)]
    return [v * g for v, g in zip(re, rows)], [v * g for v, g in zip(im, rows)]


def merge_kernel(
    bits, other, tab, tabx, taby, tabd, own_in, gain_in, table_in, out, zz, uu, mats, phases, steps, own, gain, table, sems
):
    copies = [
        pltpu.make_async_copy(source, target, sems.at[k])
        for k, (source, target) in enumerate(((own_in, own), (table_in, table), (gain_in, gain)))
    ]
    for copy in copies:
        copy.start()
    b0, b1, b2 = bits[0], bits[1], bits[2]
    prepare(tab[b0], 0, mats, phases, steps)
    prepare(tab[1 - b0], 1, mats, phases, steps)
    prepare(tab[2 + b1], 2, mats, phases, steps)
    prepare(tabx[2 + b1], 3, mats, phases, steps)
    for at, ref in ((4, tab), (5, tabx), (6, taby), (7, tabd)):
        prepare(ref[4 + b2], at, mats, phases, steps)
    run = functools.partial(stage, zz=zz, uu=uu, table=table, mats=mats, phases=phases, steps=steps)

    def blocks(ref):
        return [[ref[p, :, A * k : A * k + A] for k in range(8)] for p in range(2)]

    for copy in copies:
        copy.wait()
    first = run([blocks(own), blocks(other)], [[(0, 0), (1, 1)]])
    y = gained(first[0], gain, 0)
    second = run([y], [[(0, 2)], [(0, 3)]])
    z = [gained(v, gain, 1) for v in second]
    third = run(z, [[(0, 4)], [(1, 5)], [(0, 6)], [(1, 7)]])
    for j, v in enumerate(third):
        re, im = gained(v, gain, 2)
        for q in range(8):
            h, l = split(jnp.concatenate([re[q], im[q]], axis=1))
            out[j, q, 0:A] = h
            out[j, q, A:] = l


ROWS = A + 8


def contrib_kernel(owners, bits, cur, w0, w1, w2, w3, keep, send, acc):
    acc[...] = jnp.zeros_like(acc)
    row = lax.broadcasted_iota(jnp.int32, (8, H), 0)

    def place(owner):
        apart = owner ^ bits[3]
        return (apart & 1) * 8 + (apart >> 1)

    for j, w in enumerate((w0, w1, w2, w3)):
        for q in range(8):
            h, l = split(w[q])
            x = cur[j, q]
            c = dot(jnp.concatenate([h, h], axis=1), x) + dot(l, x[:A])
            owner = owners[j * 8 + q]
            acc[place(owner), 0:A] += c
            top = pltpu.roll(c[A - 8 :], 4, 0)
            bottom = pltpu.roll(c[:8], 4, 0)
            above = jnp.maximum(owner - 1, 0)
            below = jnp.minimum(owner + 1, 15)
            acc[place(below), A:] += jnp.where((row < 4) & (owner < 15), top, 0.0)
            acc[place(above), A:] += jnp.where((row >= 4) & (owner > 0), bottom, 0.0)
    keep[...] = acc[0:8]
    send[...] = acc[8:]


def halves_kernel(keep, taken, g0, g1, g2, g3):
    for k, ref in enumerate((g0, g1, g2, g3)):
        ref[...] = keep[2 * k : 2 * k + 2] + taken[2 * k : 2 * k + 2]


def rows_kernel(g0, r1, r2, r3, mine, theirs):
    for k, ref in enumerate((mine, theirs)):
        ref[...] = (g0[k] + r1[k]) + (r2[k] + r3[k])


def table_kernel(owners, index, weight, shift, out):
    lane = lax.broadcasted_iota(jnp.int32, (4, A), 1)
    row = jnp.zeros((4, A), jnp.int32)
    for q in range(8):
        row = jnp.where(lane == q, owners[q], row)
    for k in range(6):
        section, child = k // 2, k % 2
        out[k, 0:8] = index[section, 0, child].astype(F32)
        out[k, 8:16] = weight[section, 0, child]
        out[k, 16:20] = jnp.broadcast_to(shift[section, 0, child : child + 1, :], (4, A))
        out[k, 20:24] = row.astype(F32)


def tile_kernel(mine, taken, tile, first, last):
    total = mine[...] + taken[...]
    tile[...] = total
    re, im = total[:, :A], total[:, A:]
    lane = lax.broadcasted_iota(jnp.int32, (ROWS, A), 1)
    for ref, edge in (
        (first, jnp.where(lane < 4, re, pltpu.roll(im, 4, 1))),
        (last, jnp.where(lane < 4, pltpu.roll(re, 4, 1), pltpu.roll(im, 8, 1))),
    ):
        ref[:, :A] = edge[:A].T[:8]
        ends = jnp.concatenate([edge[A:], jnp.zeros((A - 8, A), F32)], axis=0)
        ref[:, A:] = ends.T[:8]


def filter_kernel(index, bank, tile, before, after, out, pad, moved):
    number = index[0, 0]
    sides = []
    for ref in (before, after):
        blank = jnp.zeros((A - 8, A), F32)
        main = jnp.concatenate([ref[:, :A], blank], axis=0).T
        ends = jnp.concatenate([ref[:, A:], blank], axis=0).T
        sides.append(jnp.concatenate([main, ends[:8]], axis=0))
    lane = lax.broadcasted_iota(jnp.int32, (ROWS, A), 1)
    for p in range(2):
        body = tile[:, A * p : A * p + A]
        turned = pltpu.roll(body, 4, 1)
        lead = sides[0] if p == 0 else pltpu.roll(sides[0], A - 4, 1)
        tail = pltpu.roll(sides[1], 4, 1) if p == 0 else sides[1]
        left = jnp.where(lane < 4, lead, turned)
        right = jnp.where(lane < 4, turned, tail)
        for half, value in enumerate((left, right)):
            pad[4 : 4 + A, A * half : A * half + A] = value[0:A]
            pad[0:4, A * half : A * half + A] = value[A : A + 4]
            pad[A + 4 :, A * half : A * half + A] = value[A + 4 :]
        total = jnp.zeros((A, A), F32)
        for v in range(9):
            if v:
                moved[...] = pltpu.roll(pad[...], H - v, 1)[:, :A]
            else:
                moved[...] = pad[:, :A]
            for u in range(9):
                total = total + bank[number, 9 * u + v] * moved[u : u + A, :]
        out[p] = total


def call(kernel, out_shape, in_specs, scratch=(), flops=1000000, limit=16):
    return pl.pallas_call(
        kernel,
        out_shape=out_shape,
        in_specs=in_specs,
        out_specs=jax.tree.map(lambda _: VMEM, out_shape),
        scratch_shapes=list(scratch),
        compiler_params=pltpu.CompilerParams(vmem_limit_bytes=limit << 20),
        cost_estimate=pl.CostEstimate(flops=flops, bytes_accessed=1 << 20, transcendentals=0),
    )


def struct(shape, dtype=F32):
    return jax.ShapeDtypeStruct(shape, dtype)


def swap(value, mask):
    return lax.ppermute(value, "aper", [(i, i ^ mask) for i in range(16)])


def shards(polar, tap_index, tap_weight, range_shift, range_gain, tile_owner, weights, kernel_index, bank):
    place = lax.axis_index("aper").astype(jnp.int32)
    bits = jnp.stack([place & 1, (place >> 1) & 1, (place >> 2) & 1, place])
    own_weights = weights[0, 0]
    wx, wy, wd = (swap(own_weights, mask) for mask in (2, 4, 6))
    tab = call(table_kernel, struct((6, 24, A)), [SMEM] + [VMEM] * 3, limit=60)(
        tile_owner.reshape(8), tap_index, tap_weight, range_shift
    )
    tabx, taby, tabd = (swap(tab, mask) for mask in (2, 4, 6))
    tabx, late = lax.optimization_barrier((tabx, polar))
    other = swap(late, 1)
    cur = call(
        merge_kernel,
        struct((4, 8, 2 * A, H), BF16),
        [SMEM] + [VMEM] * 5 + [HBM] * 3,
        [
            pltpu.VMEM((8, 4 * A, H), BF16),
            pltpu.VMEM((8, 4 * A, H), F32),
            pltpu.VMEM((8, 2 * A, 2 * A), BF16),
            pltpu.VMEM((8, 2, A, A), F32),
            pltpu.VMEM((8, 2, A, A), F32),
            pltpu.VMEM((2, A, N), F32),
            pltpu.VMEM((3, N), F32),
            pltpu.VMEM((2, 8, H, H), BF16),
            pltpu.SemaphoreType.DMA((3,)),
        ],
        flops=12 * 10**9,
        limit=32,
    )(bits, other, tab, tabx, taby, tabd, polar, range_gain, jnp.asarray(dft_tables()))
    owners = jnp.concatenate([t[0, 20, 0:8] for t in (tab, tabx, taby, tabd)]).astype(jnp.int32)
    keep, send = call(
        contrib_kernel,
        (struct((8, ROWS, H)), struct((8, ROWS, H))),
        [SMEM, SMEM] + [VMEM] * 5,
        [pltpu.VMEM((16, ROWS, H), F32)],
        flops=10**9,
    )(owners, bits, cur, own_weights, wx, wy, wd)
    taken = swap(send, 1)
    g0, g1, g2, g3 = call(halves_kernel, (struct((2, ROWS, H)),) * 4, [VMEM] * 2)(keep, taken)
    r1, r2, r3 = swap(g1, 4), swap(g2, 8), swap(g3, 12)
    mine, theirs = call(rows_kernel, (struct((ROWS, H)),) * 2, [VMEM] * 4)(g0, r1, r2, r3)
    taken = swap(theirs, 2)
    tile, first, last = call(
        tile_kernel, (struct((ROWS, H)), struct((8, H)), struct((8, H))), [VMEM] * 2
    )(mine, taken)
    before = lax.ppermute(last, "swath", [(i, i + 1) for i in range(7)])
    after = lax.ppermute(first, "swath", [(i + 1, i) for i in range(7)])
    return call(
        filter_kernel,
        struct((2, A, A)),
        [SMEM, SMEM] + [VMEM] * 3,
        [pltpu.VMEM((ROWS, H), F32), pltpu.VMEM((ROWS, A), F32)],
    )(kernel_index, bank, tile, before, after)


def solution(mesh):
    in_specs = (
        P(None, "aper", "swath"),
        P(None, "aper", None, None, None),
        P(None, "aper", None, None, None),
        P(None, "aper", None, None),
        P(None, "swath"),
        P("aper", "swath", None, None),
        P("aper", "swath", None, None, None),
        P("aper", "swath"),
        P(),
    )
    out_specs = P(None, "aper", "swath")
    return jax.shard_map(shards, mesh=mesh, in_specs=in_specs, out_specs=out_specs, check_vma=False)
```

```python
import functools
import math

import jax
import jax.numpy as jnp
import numpy as np
from jax import lax
from jax.experimental import pallas as pl
from jax.experimental.pallas import tpu as pltpu
from jax.sharding import PartitionSpec as P

N = 1024
H = 256
A = 128
F32 = jnp.float32
BF16 = jnp.bfloat16
VMEM = pl.BlockSpec(memory_space=pltpu.VMEM)
HBM = pl.BlockSpec(memory_space=pltpu.HBM)
SMEM = pl.BlockSpec(memory_space=pltpu.SMEM)


def dft_tables():
    r = np.arange(A)[:, None]
    out = []
    for m1 in range(8):
        m = 8 * np.arange(A)[None, :] + m1
        angle = 2.0 * np.pi * ((r * m) % N) / N
        c, s = np.cos(angle), np.sin(angle)
        forward = np.block([[c, -s], [s, c]])
        out.append(forward)
    full = np.stack(out).astype(np.float32)
    hi = full.astype(jnp.bfloat16)
    lo = (full - hi.astype(np.float32)).astype(jnp.bfloat16)
    return np.stack([hi, lo])


def split(x):
    hi = x.astype(BF16)
    return hi, (x - hi.astype(F32)).astype(BF16)


def dot(a, b):
    return jnp.dot(a, b, preferred_element_type=F32)


def quarter_turns(re, im, sign):
    ar, ai = re[0] + re[2], im[0] + im[2]
    br, bi = re[0] - re[2], im[0] - im[2]
    cr, ci = re[1] + re[3], im[1] + im[3]
    dr, di = re[1] - re[3], im[1] - im[3]
    if sign > 0:
        er, ei = -di, dr
    else:
        er, ei = di, -dr
    return [ar + cr, br + er, ar - cr, br - er], [ai + ci, bi + ei, ai - ci, bi - ei]


def eighth_turns(re, im, sign):
    er, ei = quarter_turns(re[0::2], im[0::2], sign)
    br, bi = quarter_turns(re[1::2], im[1::2], sign)
    root = F32(math.sqrt(0.5))
    if sign > 0:
        tr = [br[0], (br[1] - bi[1]) * root, -bi[2], (br[3] + bi[3]) * -root]
        ti = [bi[0], (bi[1] + br[1]) * root, br[2], (br[3] - bi[3]) * root]
    else:
        tr = [br[0], (br[1] + bi[1]) * root, bi[2], (bi[3] - br[3]) * root]
        ti = [bi[0], (bi[1] - br[1]) * root, -br[2], (bi[3] + br[3]) * -root]
    out_re = [e + t for e, t in zip(er, tr)] + [e - t for e, t in zip(er, tr)]
    out_im = [e + t for e, t in zip(ei, ti)] + [e - t for e, t in zip(ei, ti)]
    return out_re, out_im


def sincos_turns(t):
    t = t - jnp.round(t)
    q = jnp.round(t * 4.0)
    y = (t - q * 0.25) * F32(2.0 * math.pi)
    y2 = y * y
    s = y * (1.0 + y2 * (-1.0 / 6 + y2 * (1.0 / 120 + y2 * (-1.0 / 5040 + y2 * (1.0 / 362880)))))
    c = 1.0 + y2 * (-0.5 + y2 * (1.0 / 24 + y2 * (-1.0 / 720 + y2 * (1.0 / 40320 - y2 * (1.0 / 3628800)))))
    odd = jnp.abs(q) == 1.0
    half = jnp.abs(q) == 2.0
    sign = jnp.where(q < 0, -1.0, 1.0)
    cc = jnp.where(odd, -sign * s, jnp.where(half, -c, c))
    ss = jnp.where(odd, sign * c, jnp.where(half, -s, s))
    return cc, ss


def prepare(tab, at, mats, phases, steps):
    rows = lax.broadcasted_iota(jnp.int32, (A, A), 0).astype(F32)
    total = jnp.zeros((A, A), F32)
    for t in range(8):
        total = total + jnp.where(rows == tab[t : t + 1, :], tab[8 + t : 9 + t, :], 0.0)
    hi, lo = split(total.T)
    mats[at, 0:A, 0:A] = hi
    mats[at, 0:A, A:] = hi
    mats[at, A:, 0:A] = lo
    mats[at, A:, A:] = jnp.zeros((A, A), BF16)
    shift = jnp.broadcast_to(tab[16:17, :], (A, A)).T
    lane = lax.broadcasted_iota(jnp.int32, (A, A), 1)
    lane = jnp.where(lane < A // 2, lane, lane - A).astype(F32)
    c, s = sincos_turns(shift * lane * F32(-8.0 / N))
    phases[at, 0] = c
    phases[at, 1] = s
    c1, s1 = sincos_turns(shift * F32(-1.0 / N))
    steps[at, 0] = c1
    steps[at, 1] = s1


def product(lhs, table, m1, rows, dims):
    def by(a, b):
        return lax.dot_general(a, b, (dims, ((), ())), preferred_element_type=F32)

    both = by(lhs, table[0, m1])
    return both[:rows] + both[rows:] + by(lhs[:rows], table[1, m1])


def stage(inputs, plan, zz, uu, table, mats, phases, steps):
    n_in, n_out = len(inputs), len(plan)
    rows_in, rows_out = n_in * A, n_out * A
    for which, (re, im) in enumerate(inputs):
        zr, zi = eighth_turns(re, im, -1)
        for m1 in range(8):
            h, l = split(jnp.concatenate([zr[m1], zi[m1]], axis=1))
            zz[m1, which * A : which * A + A] = h
            zz[m1, rows_in + which * A : rows_in + which * A + A] = l
    turns = {at: (phases[at, 0], phases[at, 1]) for terms in plan for _, at in terms}
    for m1 in range(8):
        x = product(zz[m1, : 2 * rows_in], table, m1, rows_in, ((1,), (0,)))
        h, l = split(x)
        stacked = [
            jnp.concatenate([h[which * A : which * A + A], l[which * A : which * A + A]], axis=0)
            for which in range(n_in)
        ]
        highs, lows = [], []
        for terms in plan:
            mr = mi = None
            for which, at in terms:
                y = dot(mats[at], stacked[which])
                y = y[:A] + y[A:]
                yr, yi = y[:, :A], y[:, A:]
                c, s = turns[at]
                tr, ti = c * yr - s * yi, c * yi + s * yr
                mr, mi = (tr, ti) if mr is None else (mr + tr, mi + ti)
                if m1 < 7:
                    c1, s1 = steps[at, 0], steps[at, 1]
                    turns[at] = (c * c1 - s * s1, c * s1 + s * c1)
            h, l = split(jnp.concatenate([mr, mi], axis=1))
            highs.append(h)
            lows.append(l)
        lhs = jnp.concatenate(highs + lows, axis=0)
        uu[m1, :rows_out] = product(lhs, table, m1, rows_out, ((1,), (1,)))
    out = []
    for which in range(n_out):
        base = which * A
        re = [uu[m1, base : base + A, :A] for m1 in range(8)]
        im = [uu[m1, base : base + A, A:] for m1 in range(8)]
        out.append(eighth_turns(re, im, 1))
    return out


def gained(blocks, gain, section):
    re, im = blocks
    rows = [gain[6, 8 * section + k : 8 * section + k + 1, :] for k in range(8)]
    return [v * g for v, g in zip(re, rows)], [v * g for v, g in zip(im, rows)]


def merge_kernel(
    bits, other, tab, tabx, taby, tabd, own_in, table_in, out, zz, uu, mats, phases, steps, own, table, sems
):
    copies = [
        pltpu.make_async_copy(source, target, sems.at[k])
        for k, (source, target) in enumerate(((own_in, own), (table_in, table)))
    ]
    for copy in copies:
        copy.start()
    b0, b1, b2 = bits[0], bits[1], bits[2]
    prepare(tab[b0], 0, mats, phases, steps)
    prepare(tab[1 - b0], 1, mats, phases, steps)
    prepare(tab[2 + b1], 2, mats, phases, steps)
    prepare(tabx[2 + b1], 3, mats, phases, steps)
    for at, ref in ((4, tab), (5, tabx), (6, taby), (7, tabd)):
        prepare(ref[4 + b2], at, mats, phases, steps)
    run = functools.partial(stage, zz=zz, uu=uu, table=table, mats=mats, phases=phases, steps=steps)

    def blocks(ref):
        return [[ref[p, :, A * k : A * k + A] for k in range(8)] for p in range(2)]

    for copy in copies:
        copy.wait()
    first = run([blocks(own), blocks(other)], [[(0, 0), (1, 1)]])
    y = gained(first[0], tab, 0)
    second = run([y], [[(0, 2)], [(0, 3)]])
    z = [gained(v, tab, 1) for v in second]
    third = run(z, [[(0, 4)], [(1, 5)], [(0, 6)], [(1, 7)]])
    for j, v in enumerate(third):
        re, im = gained(v, tab, 2)
        for q in range(8):
            h, l = split(jnp.concatenate([re[q], im[q]], axis=1))
            out[j, q, 0:A] = h
            out[j, q, A:] = l


ROWS = A + 8


def contrib_kernel(owners, bits, cur, w0, w1, w2, w3, keep, send, acc):
    acc[...] = jnp.zeros_like(acc)
    row = lax.broadcasted_iota(jnp.int32, (8, H), 0)

    def place(owner):
        apart = owner ^ bits[3]
        return (apart & 1) * 8 + (apart >> 1)

    for j, w in enumerate((w0, w1, w2, w3)):
        for q in range(8):
            h, l = split(w[q])
            x = cur[j, q]
            c = dot(jnp.concatenate([h, h], axis=1), x) + dot(l, x[:A])
            owner = owners[j * 8 + q]
            acc[place(owner), 0:A] += c
            top = pltpu.roll(c[A - 8 :], 4, 0)
            bottom = pltpu.roll(c[:8], 4, 0)
            above = jnp.maximum(owner - 1, 0)
            below = jnp.minimum(owner + 1, 15)
            acc[place(below), A:] += jnp.where((row < 4) & (owner < 15), top, 0.0)
            acc[place(above), A:] += jnp.where((row >= 4) & (owner > 0), bottom, 0.0)
    keep[...] = acc[0:8]
    send[...] = acc[8:]


def halves_kernel(keep, taken, g0, g1, g2, g3):
    for k, ref in enumerate((g0, g1, g2, g3)):
        ref[...] = keep[2 * k : 2 * k + 2] + taken[2 * k : 2 * k + 2]


def rows_kernel(g0, r1, r2, r3, mine, theirs):
    for k, ref in enumerate((mine, theirs)):
        ref[...] = (g0[k] + r1[k]) + (r2[k] + r3[k])


def table_kernel(owners, index, weight, shift, gain, out):
    lane = lax.broadcasted_iota(jnp.int32, (4, A), 1)
    row = jnp.zeros((4, A), jnp.int32)
    for q in range(8):
        row = jnp.where(lane == q, owners[q], row)
    for k in range(6):
        section, child = k // 2, k % 2
        out[k, 0:8] = index[section, 0, child].astype(F32)
        out[k, 8:16] = weight[section, 0, child]
        out[k, 16:20] = jnp.broadcast_to(shift[section, 0, child : child + 1, :], (4, A))
        out[k, 20:24] = row.astype(F32)
    for section in range(3):
        for k in range(8):
            at = 8 * section + k
            out[6, at : at + 1] = gain[section : section + 1, A * k : A * k + A] * F32(1.0 / N)


def tile_kernel(mine, taken, tile, first, last):
    total = mine[...] + taken[...]
    tile[...] = total
    re, im = total[:, :A], total[:, A:]
    lane = lax.broadcasted_iota(jnp.int32, (ROWS, A), 1)
    for ref, edge in (
        (first, jnp.where(lane < 4, re, pltpu.roll(im, 4, 1))),
        (last, jnp.where(lane < 4, pltpu.roll(re, 4, 1), pltpu.roll(im, 8, 1))),
    ):
        ref[:, :A] = edge[:A].T[:8]
        ends = jnp.concatenate([edge[A:], jnp.zeros((A - 8, A), F32)], axis=0)
        ref[:, A:] = ends.T[:8]


def filter_kernel(index, bank, tile, out, pad, moved, lines):
    number = index[0, 0]
    lane = lax.broadcasted_iota(jnp.int32, (ROWS, A), 1)
    for p in range(2):
        body = tile[:, A * p : A * p + A]
        turned = pltpu.roll(body, 4, 1)
        left = jnp.where(lane < 4, 0.0, turned)
        right = jnp.where(lane < 4, turned, 0.0)
        for half, value in enumerate((left, right)):
            pad[4 : 4 + A, A * half : A * half + A] = value[0:A]
            pad[0:4, A * half : A * half + A] = value[A : A + 4]
            pad[A + 4 :, A * half : A * half + A] = value[A + 4 :]
        for v in range(9):
            moved[v] = pltpu.roll(pad[...], H - v, 1)[:, :A] if v else pad[:, :A]
        total = jnp.zeros((A, A), F32)
        for u in range(9):
            line = bank[number, 9 * u] * moved[0]
            for v in range(1, 9):
                line = line + bank[number, 9 * u + v] * moved[v]
            lines[p, u] = line
            total = total + lines[p, u, u : u + A, :]
        out[p] = total


def side_kernel(index, bank, main, before, after, out):
    number = index[0, 0]
    lane = lax.broadcasted_iota(jnp.int32, (8, H), 1)
    row = lax.broadcasted_iota(jnp.int32, (8, A), 0)
    sums = []
    for ref, first in ((before, 0), (after, 5)):
        value = ref[...]
        ends = pltpu.roll(value, A, 1)
        spread = jnp.where(lane < 4, ends, jnp.where(lane < A + 4, pltpu.roll(value, 4, 1), value))
        turned = [pltpu.roll(spread, H - u, 1)[:, :A] if u else spread[:, :A] for u in range(9)]
        total = jnp.zeros((8, A), F32)
        for v in range(first, first + 4):
            line = bank[number, v] * turned[0]
            for u in range(1, 9):
                line = line + bank[number, 9 * u + v] * turned[u]
            if first == 0:
                line = pltpu.roll(line, 8 - v, 0) if v else line
                total = total + jnp.where(row % 4 + v < 4, line, 0.0)
            else:
                line = pltpu.roll(line, 8 - v, 0) if v < 8 else line
                total = total + jnp.where(row % 4 >= 8 - v, line, 0.0)
        sums.append(total)
    blank = jnp.zeros((A - 16, A), F32)
    for p in range(2):
        head = sums[0] if p == 0 else pltpu.roll(sums[0], 4, 0)
        tail = sums[1] if p == 1 else pltpu.roll(sums[1], 4, 0)
        head = jnp.where(row < 4, head, 0.0)
        tail = jnp.where(row >= 4, tail, 0.0)
        out[p] = main[p] + jnp.concatenate([head, blank, tail], axis=0).T


def call(kernel, out_shape, in_specs, scratch=(), flops=1000000, limit=16):
    return pl.pallas_call(
        kernel,
        out_shape=out_shape,
        in_specs=in_specs,
        out_specs=jax.tree.map(lambda _: VMEM, out_shape),
        scratch_shapes=list(scratch),
        compiler_params=pltpu.CompilerParams(vmem_limit_bytes=limit << 20),
        cost_estimate=pl.CostEstimate(flops=flops, bytes_accessed=1 << 20, transcendentals=0),
    )


def struct(shape, dtype=F32):
    return jax.ShapeDtypeStruct(shape, dtype)


def swap(value, mask):
    return lax.ppermute(value, "aper", [(i, i ^ mask) for i in range(16)])


def shards(polar, tap_index, tap_weight, range_shift, range_gain, tile_owner, weights, kernel_index, bank):
    place = lax.axis_index("aper").astype(jnp.int32)
    bits = jnp.stack([place & 1, (place >> 1) & 1, (place >> 2) & 1, place])
    own_weights = weights[0, 0]
    wx, wy, wd = (swap(own_weights, mask) for mask in (2, 4, 6))
    tab = call(table_kernel, struct((7, 24, A)), [SMEM] + [VMEM] * 4, limit=60)(
        tile_owner.reshape(8), tap_index, tap_weight, range_shift, range_gain
    )
    tabx, taby, tabd = (swap(tab, mask) for mask in (2, 4, 6))
    tabx, late = lax.optimization_barrier((tabx, polar))
    other = swap(late, 1)
    cur = call(
        merge_kernel,
        struct((4, 8, 2 * A, H), BF16),
        [SMEM] + [VMEM] * 5 + [HBM] * 2,
        [
            pltpu.VMEM((8, 4 * A, H), BF16),
            pltpu.VMEM((8, 4 * A, H), F32),
            pltpu.VMEM((8, 2 * A, 2 * A), BF16),
            pltpu.VMEM((8, 2, A, A), F32),
            pltpu.VMEM((8, 2, A, A), F32),
            pltpu.VMEM((2, A, N), F32),
            pltpu.VMEM((2, 8, H, H), BF16),
            pltpu.SemaphoreType.DMA((2,)),
        ],
        flops=12 * 10**9,
        limit=32,
    )(bits, other, tab, tabx, taby, tabd, polar, jnp.asarray(dft_tables()))
    owners = jnp.concatenate([t[0, 20, 0:8] for t in (tab, tabx, taby, tabd)]).astype(jnp.int32)
    keep, send = call(
        contrib_kernel,
        (struct((8, ROWS, H)), struct((8, ROWS, H))),
        [SMEM, SMEM] + [VMEM] * 5,
        [pltpu.VMEM((16, ROWS, H), F32)],
        flops=10**9,
    )(owners, bits, cur, own_weights, wx, wy, wd)
    taken = swap(send, 1)
    g0, g1, g2, g3 = call(halves_kernel, (struct((2, ROWS, H)),) * 4, [VMEM] * 2)(keep, taken)
    r1, r2, r3 = swap(g1, 4), swap(g2, 8), swap(g3, 12)
    mine, theirs = call(rows_kernel, (struct((ROWS, H)),) * 2, [VMEM] * 4)(g0, r1, r2, r3)
    taken = swap(theirs, 2)
    tile, first, last = call(
        tile_kernel, (struct((ROWS, H)), struct((8, H)), struct((8, H))), [VMEM] * 2
    )(mine, taken)
    before = lax.ppermute(last, "swath", [(i, i + 1) for i in range(7)])
    after = lax.ppermute(first, "swath", [(i + 1, i) for i in range(7)])
    main = call(
        filter_kernel,
        struct((2, A, A)),
        [SMEM, SMEM, VMEM],
        [
            pltpu.VMEM((ROWS, H), F32),
            pltpu.VMEM((9, ROWS, A), F32),
            pltpu.VMEM((2, 9, ROWS, A), F32),
        ],
        flops=10**9,
    )(kernel_index, bank, tile)
    return call(side_kernel, struct((2, A, A)), [SMEM, SMEM] + [VMEM] * 3)(kernel_index, bank, main, before, after)


def solution(mesh):
    in_specs = (
        P(None, "aper", "swath"),
        P(None, "aper", None, None, None),
        P(None, "aper", None, None, None),
        P(None, "aper", None, None),
        P(None, "swath"),
        P("aper", "swath", None, None),
        P("aper", "swath", None, None, None),
        P("aper", "swath"),
        P(),
    )
    out_specs = P(None, "aper", "swath")
    return jax.shard_map(shards, mesh=mesh, in_specs=in_specs, out_specs=out_specs, check_vma=False)
```

```python
import functools
import math

import jax
import jax.numpy as jnp
import numpy as np
from jax import lax
from jax.experimental import pallas as pl
from jax.experimental.pallas import tpu as pltpu
from jax.sharding import PartitionSpec as P

N = 1024
H = 256
A = 128
F32 = jnp.float32
BF16 = jnp.bfloat16
VMEM = pl.BlockSpec(memory_space=pltpu.VMEM)
HBM = pl.BlockSpec(memory_space=pltpu.HBM)
SMEM = pl.BlockSpec(memory_space=pltpu.SMEM)


def dft_tables():
    r = np.arange(A)[:, None]
    out = []
    for m1 in range(8):
        m = 8 * np.arange(A)[None, :] + m1
        angle = 2.0 * np.pi * ((r * m) % N) / N
        c, s = np.cos(angle), np.sin(angle)
        forward = np.block([[c, -s], [s, c]])
        out.append(forward)
    full = np.stack(out).astype(np.float32)
    hi = full.astype(jnp.bfloat16)
    lo = (full - hi.astype(np.float32)).astype(jnp.bfloat16)
    return np.stack([hi, lo])


def split(x):
    hi = x.astype(BF16)
    return hi, (x - hi.astype(F32)).astype(BF16)


def dot(a, b):
    return jnp.dot(a, b, preferred_element_type=F32)


def quarter_turns(re, im, sign):
    ar, ai = re[0] + re[2], im[0] + im[2]
    br, bi = re[0] - re[2], im[0] - im[2]
    cr, ci = re[1] + re[3], im[1] + im[3]
    dr, di = re[1] - re[3], im[1] - im[3]
    if sign > 0:
        er, ei = -di, dr
    else:
        er, ei = di, -dr
    return [ar + cr, br + er, ar - cr, br - er], [ai + ci, bi + ei, ai - ci, bi - ei]


def eighth_turns(re, im, sign):
    er, ei = quarter_turns(re[0::2], im[0::2], sign)
    br, bi = quarter_turns(re[1::2], im[1::2], sign)
    root = F32(math.sqrt(0.5))
    if sign > 0:
        tr = [br[0], (br[1] - bi[1]) * root, -bi[2], (br[3] + bi[3]) * -root]
        ti = [bi[0], (bi[1] + br[1]) * root, br[2], (br[3] - bi[3]) * root]
    else:
        tr = [br[0], (br[1] + bi[1]) * root, bi[2], (bi[3] - br[3]) * root]
        ti = [bi[0], (bi[1] - br[1]) * root, -br[2], (bi[3] + br[3]) * -root]
    out_re = [e + t for e, t in zip(er, tr)] + [e - t for e, t in zip(er, tr)]
    out_im = [e + t for e, t in zip(ei, ti)] + [e - t for e, t in zip(ei, ti)]
    return out_re, out_im


def sincos_turns(t):
    t = t - jnp.round(t)
    q = jnp.round(t * 4.0)
    y = (t - q * 0.25) * F32(2.0 * math.pi)
    y2 = y * y
    s = y * (1.0 + y2 * (-1.0 / 6 + y2 * (1.0 / 120 + y2 * (-1.0 / 5040 + y2 * (1.0 / 362880)))))
    c = 1.0 + y2 * (-0.5 + y2 * (1.0 / 24 + y2 * (-1.0 / 720 + y2 * (1.0 / 40320 - y2 * (1.0 / 3628800)))))
    odd = jnp.abs(q) == 1.0
    half = jnp.abs(q) == 2.0
    sign = jnp.where(q < 0, -1.0, 1.0)
    cc = jnp.where(odd, -sign * s, jnp.where(half, -c, c))
    ss = jnp.where(odd, sign * c, jnp.where(half, -s, s))
    return cc, ss


def prepare(tab, at, mats, phases, steps):
    rows = lax.broadcasted_iota(jnp.int32, (A, A), 0).astype(F32)
    total = jnp.zeros((A, A), F32)
    for t in range(8):
        total = total + jnp.where(rows == tab[t : t + 1, :], tab[8 + t : 9 + t, :], 0.0)
    hi, lo = split(total.T)
    mats[at, 0:A, 0:A] = hi
    mats[at, 0:A, A:] = hi
    mats[at, A:, 0:A] = lo
    mats[at, A:, A:] = jnp.zeros((A, A), BF16)
    shift = jnp.broadcast_to(tab[16:17, :], (A, A)).T
    lane = lax.broadcasted_iota(jnp.int32, (A, A), 1)
    lane = jnp.where(lane < A // 2, lane, lane - A).astype(F32)
    c, s = sincos_turns(shift * lane * F32(-8.0 / N))
    phases[at, 0] = c
    phases[at, 1] = s
    c1, s1 = sincos_turns(shift * F32(-1.0 / N))
    steps[at, 0] = c1
    steps[at, 1] = s1


def product(lhs, table, m1, rows, dims):
    def by(a, b):
        return lax.dot_general(a, b, (dims, ((), ())), preferred_element_type=F32)

    both = by(lhs, table[0, m1])
    return both[:rows] + both[rows:] + by(lhs[:rows], table[1, m1])


def stage(inputs, plan, zz, uu, table, mats, phases, steps):
    n_in, n_out = len(inputs), len(plan)
    rows_in, rows_out = n_in * A, n_out * A
    for which, (re, im) in enumerate(inputs):
        zr, zi = eighth_turns(re, im, -1)
        for m1 in range(8):
            h, l = split(jnp.concatenate([zr[m1], zi[m1]], axis=1))
            zz[m1, which * A : which * A + A] = h
            zz[m1, rows_in + which * A : rows_in + which * A + A] = l
    turns = {at: (phases[at, 0], phases[at, 1]) for terms in plan for _, at in terms}
    for m1 in range(8):
        x = product(zz[m1, : 2 * rows_in], table, m1, rows_in, ((1,), (0,)))
        h, l = split(x)
        stacked = [
            jnp.concatenate([h[which * A : which * A + A], l[which * A : which * A + A]], axis=0)
            for which in range(n_in)
        ]
        highs, lows = [], []
        for terms in plan:
            mr = mi = None
            for which, at in terms:
                y = dot(mats[at], stacked[which])
                y = y[:A] + y[A:]
                yr, yi = y[:, :A], y[:, A:]
                c, s = turns[at]
                tr, ti = c * yr - s * yi, c * yi + s * yr
                mr, mi = (tr, ti) if mr is None else (mr + tr, mi + ti)
                if m1 < 7:
                    c1, s1 = steps[at, 0], steps[at, 1]
                    turns[at] = (c * c1 - s * s1, c * s1 + s * c1)
            h, l = split(jnp.concatenate([mr, mi], axis=1))
            highs.append(h)
            lows.append(l)
        lhs = jnp.concatenate(highs + lows, axis=0)
        uu[m1, :rows_out] = product(lhs, table, m1, rows_out, ((1,), (1,)))
    out = []
    for which in range(n_out):
        base = which * A
        re = [uu[m1, base : base + A, :A] for m1 in range(8)]
        im = [uu[m1, base : base + A, A:] for m1 in range(8)]
        out.append(eighth_turns(re, im, 1))
    return out


def gained(blocks, gain, section):
    re, im = blocks
    rows = [gain[6, 8 * section + k : 8 * section + k + 1, :] for k in range(8)]
    return [v * g for v, g in zip(re, rows)], [v * g for v, g in zip(im, rows)]


def merge_kernel(
    bits, other, tab, tabx, taby, tabd, own_in, table_in, out, zz, uu, mats, phases, steps, own, table, sems
):
    copies = [
        pltpu.make_async_copy(source, target, sems.at[k])
        for k, (source, target) in enumerate(((own_in, own), (table_in, table)))
    ]
    for copy in copies:
        copy.start()
    b0, b1, b2 = bits[0], bits[1], bits[2]
    prepare(tab[b0], 0, mats, phases, steps)
    prepare(tab[1 - b0], 1, mats, phases, steps)
    prepare(tab[2 + b1], 2, mats, phases, steps)
    prepare(tabx[b1], 3, mats, phases, steps)
    for at, ref, first_row in ((4, tab, 4), (5, tabx, 2), (6, taby, 2), (7, tabd, 2)):
        prepare(ref[first_row + b2], at, mats, phases, steps)
    run = functools.partial(stage, zz=zz, uu=uu, table=table, mats=mats, phases=phases, steps=steps)

    def blocks(ref):
        return [[ref[p, :, A * k : A * k + A] for k in range(8)] for p in range(2)]

    for copy in copies:
        copy.wait()
    first = run([blocks(own), blocks(other)], [[(0, 0), (1, 1)]])
    y = gained(first[0], tab, 0)
    second = run([y], [[(0, 2)], [(0, 3)]])
    z = [gained(v, tab, 1) for v in second]
    third = run(z, [[(0, 4)], [(1, 5)], [(0, 6)], [(1, 7)]])
    for j, v in enumerate(third):
        re, im = gained(v, tab, 2)
        for q in range(8):
            h, l = split(jnp.concatenate([re[q], im[q]], axis=1))
            out[j, q, 0:A] = h
            out[j, q, A:] = l


ROWS = A + 8


def contrib_kernel(owners, bits, cur, w0, w1, w2, w3, keep, send, acc):
    acc[...] = jnp.zeros_like(acc)
    row = lax.broadcasted_iota(jnp.int32, (8, H), 0)

    def place(owner):
        apart = owner ^ bits[3]
        return (apart & 1) * 8 + (apart >> 1)

    for j, w in enumerate((w0, w1, w2, w3)):
        for q in range(8):
            h, l = split(w[q])
            x = cur[j, q]
            c = dot(jnp.concatenate([h, h], axis=1), x) + dot(l, x[:A])
            owner = owners[j * 8 + q]
            acc[place(owner), 0:A] += c
            top = pltpu.roll(c[A - 8 :], 4, 0)
            bottom = pltpu.roll(c[:8], 4, 0)
            above = jnp.maximum(owner - 1, 0)
            below = jnp.minimum(owner + 1, 15)
            acc[place(below), A:] += jnp.where((row < 4) & (owner < 15), top, 0.0)
            acc[place(above), A:] += jnp.where((row >= 4) & (owner > 0), bottom, 0.0)
    keep[...] = acc[0:8]
    send[...] = acc[8:]


def halves_kernel(keep, taken, g0, g1, g2, g3):
    for k, ref in enumerate((g0, g1, g2, g3)):
        ref[...] = keep[2 * k : 2 * k + 2] + taken[2 * k : 2 * k + 2]


def rows_kernel(g0, r1, r2, r3, mine, theirs):
    for k, ref in enumerate((mine, theirs)):
        ref[...] = (g0[k] + r1[k]) + (r2[k] + r3[k])


def table_kernel(owners, index, weight, shift, gain, out, sent):
    lane = lax.broadcasted_iota(jnp.int32, (4, A), 1)
    row = jnp.zeros((4, A), jnp.int32)
    for q in range(8):
        row = jnp.where(lane == q, owners[q], row)
    for k in range(6):
        section, child = k // 2, k % 2
        out[k, 0:8] = index[section, 0, child].astype(F32)
        out[k, 8:16] = weight[section, 0, child]
        out[k, 16:20] = jnp.broadcast_to(shift[section, 0, child : child + 1, :], (4, A))
        out[k, 20:24] = row.astype(F32)
    sent[...] = out[2:6]
    for section in range(3):
        for k in range(8):
            at = 8 * section + k
            out[6, at : at + 1] = gain[section : section + 1, A * k : A * k + A] * F32(1.0 / N)


def tile_kernel(mine, taken, tile, first, last):
    total = mine[...] + taken[...]
    tile[...] = total
    re, im = total[:, :A], total[:, A:]
    lane = lax.broadcasted_iota(jnp.int32, (ROWS, A), 1)
    for ref, edge in (
        (first, jnp.where(lane < 4, re, pltpu.roll(im, 4, 1))),
        (last, jnp.where(lane < 4, pltpu.roll(re, 4, 1), pltpu.roll(im, 8, 1))),
    ):
        ref[:, :A] = edge[:A].T[:8]
        ends = jnp.concatenate([edge[A:], jnp.zeros((A - 8, A), F32)], axis=0)
        ref[:, A:] = ends.T[:8]


def filter_kernel(index, bank, tile, out, pad, moved, lines):
    number = index[0, 0]
    lane = lax.broadcasted_iota(jnp.int32, (ROWS, A), 1)
    for p in range(2):
        body = tile[:, A * p : A * p + A]
        turned = pltpu.roll(body, 4, 1)
        left = jnp.where(lane < 4, 0.0, turned)
        right = jnp.where(lane < 4, turned, 0.0)
        for half, value in enumerate((left, right)):
            pad[4 : 4 + A, A * half : A * half + A] = value[0:A]
            pad[0:4, A * half : A * half + A] = value[A : A + 4]
            pad[A + 4 :, A * half : A * half + A] = value[A + 4 :]
        for v in range(9):
            moved[v] = pltpu.roll(pad[...], H - v, 1)[:, :A] if v else pad[:, :A]
        total = jnp.zeros((A, A), F32)
        for u in range(9):
            line = bank[number, 9 * u] * moved[0]
            for v in range(1, 9):
                line = line + bank[number, 9 * u + v] * moved[v]
            lines[p, u] = line
            total = total + lines[p, u, u : u + A, :]
        out[p] = total


def side_kernel(index, bank, main, before, after, out):
    number = index[0, 0]
    lane = lax.broadcasted_iota(jnp.int32, (8, H), 1)
    row = lax.broadcasted_iota(jnp.int32, (8, A), 0)
    sums = []
    for ref, first in ((before, 0), (after, 5)):
        value = ref[...]
        ends = pltpu.roll(value, A, 1)
        spread = jnp.where(lane < 4, ends, jnp.where(lane < A + 4, pltpu.roll(value, 4, 1), value))
        turned = [pltpu.roll(spread, H - u, 1)[:, :A] if u else spread[:, :A] for u in range(9)]
        total = jnp.zeros((8, A), F32)
        for v in range(first, first + 4):
            line = bank[number, v] * turned[0]
            for u in range(1, 9):
                line = line + bank[number, 9 * u + v] * turned[u]
            if first == 0:
                line = pltpu.roll(line, 8 - v, 0) if v else line
                total = total + jnp.where(row % 4 + v < 4, line, 0.0)
            else:
                line = pltpu.roll(line, 8 - v, 0) if v < 8 else line
                total = total + jnp.where(row % 4 >= 8 - v, line, 0.0)
        sums.append(total)
    blank = jnp.zeros((A - 16, A), F32)
    for p in range(2):
        head = sums[0] if p == 0 else pltpu.roll(sums[0], 4, 0)
        tail = sums[1] if p == 1 else pltpu.roll(sums[1], 4, 0)
        head = jnp.where(row < 4, head, 0.0)
        tail = jnp.where(row >= 4, tail, 0.0)
        out[p] = main[p] + jnp.concatenate([head, blank, tail], axis=0).T


def call(kernel, out_shape, in_specs, scratch=(), flops=1000000, limit=16):
    return pl.pallas_call(
        kernel,
        out_shape=out_shape,
        in_specs=in_specs,
        out_specs=jax.tree.map(lambda _: VMEM, out_shape),
        scratch_shapes=list(scratch),
        compiler_params=pltpu.CompilerParams(vmem_limit_bytes=limit << 20),
        cost_estimate=pl.CostEstimate(flops=flops, bytes_accessed=1 << 20, transcendentals=0),
    )


def struct(shape, dtype=F32):
    return jax.ShapeDtypeStruct(shape, dtype)


def swap(value, mask):
    return lax.ppermute(value, "aper", [(i, i ^ mask) for i in range(16)])


def shards(polar, tap_index, tap_weight, range_shift, range_gain, tile_owner, weights, kernel_index, bank):
    place = lax.axis_index("aper").astype(jnp.int32)
    bits = jnp.stack([place & 1, (place >> 1) & 1, (place >> 2) & 1, place])
    own_weights = weights[0, 0]
    wx, wy, wd = (swap(own_weights, mask) for mask in (2, 4, 6))
    tab, sent = call(table_kernel, (struct((7, 24, A)), struct((4, 24, A))), [SMEM] + [VMEM] * 4, limit=60)(
        tile_owner.reshape(8), tap_index, tap_weight, range_shift, range_gain
    )
    tabx, taby, tabd = (swap(sent, mask) for mask in (2, 4, 6))
    tabx, late = lax.optimization_barrier((tabx, polar))
    other = swap(late, 1)
    cur = call(
        merge_kernel,
        struct((4, 8, 2 * A, H), BF16),
        [SMEM] + [VMEM] * 5 + [HBM] * 2,
        [
            pltpu.VMEM((8, 4 * A, H), BF16),
            pltpu.VMEM((8, 4 * A, H), F32),
            pltpu.VMEM((8, 2 * A, 2 * A), BF16),
            pltpu.VMEM((8, 2, A, A), F32),
            pltpu.VMEM((8, 2, A, A), F32),
            pltpu.VMEM((2, A, N), F32),
            pltpu.VMEM((2, 8, H, H), BF16),
            pltpu.SemaphoreType.DMA((2,)),
        ],
        flops=12 * 10**9,
        limit=32,
    )(bits, other, tab, tabx, taby, tabd, polar, jnp.asarray(dft_tables()))
    owners = jnp.concatenate([t[0, 20, 0:8] for t in (tab, tabx, taby, tabd)]).astype(jnp.int32)
    keep, send = call(
        contrib_kernel,
        (struct((8, ROWS, H)), struct((8, ROWS, H))),
        [SMEM, SMEM] + [VMEM] * 5,
        [pltpu.VMEM((16, ROWS, H), F32)],
        flops=10**9,
    )(owners, bits, cur, own_weights, wx, wy, wd)
    taken = swap(send, 1)
    g0, g1, g2, g3 = call(halves_kernel, (struct((2, ROWS, H)),) * 4, [VMEM] * 2)(keep, taken)
    r1, r2, r3 = swap(g1, 4), swap(g2, 8), swap(g3, 12)
    mine, theirs = call(rows_kernel, (struct((ROWS, H)),) * 2, [VMEM] * 4)(g0, r1, r2, r3)
    taken = swap(theirs, 2)
    tile, first, last = call(
        tile_kernel, (struct((ROWS, H)), struct((8, H)), struct((8, H))), [VMEM] * 2
    )(mine, taken)
    before = lax.ppermute(last, "swath", [(i, i + 1) for i in range(7)])
    after = lax.ppermute(first, "swath", [(i + 1, i) for i in range(7)])
    main = call(
        filter_kernel,
        struct((2, A, A)),
        [SMEM, SMEM, VMEM],
        [
            pltpu.VMEM((ROWS, H), F32),
            pltpu.VMEM((9, ROWS, A), F32),
            pltpu.VMEM((2, 9, ROWS, A), F32),
        ],
        flops=10**9,
    )(kernel_index, bank, tile)
    return call(side_kernel, struct((2, A, A)), [SMEM, SMEM] + [VMEM] * 3)(kernel_index, bank, main, before, after)


def solution(mesh):
    in_specs = (
        P(None, "aper", "swath"),
        P(None, "aper", None, None, None),
        P(None, "aper", None, None, None),
        P(None, "aper", None, None),
        P(None, "swath"),
        P("aper", "swath", None, None),
        P("aper", "swath", None, None, None),
        P("aper", "swath"),
        P(),
    )
    out_specs = P(None, "aper", "swath")
    return jax.shard_map(shards, mesh=mesh, in_specs=in_specs, out_specs=out_specs, check_vma=False)
```
